256 devices in a mesh: depth: 32 (over x, y, core), tile: 8 (over z).
Axes of the slice: x: 4, y: 4, z: 8, core: 2. Of those that a mesh axis runs over, the one named last changes fastest.
Arguments:
- pressure_old: float32 [256, 512, 1024], P('depth', 'tile'), may hold values from -6 to 6
- pressure_now: float32 [256, 512, 1024], P('depth', 'tile'), may hold values from -6 to 6
- solid_flags: int32 [256, 512, 1024], P('depth', 'tile'), may hold values 0 or 1
Outputs:
- pressure_mid: float32 [256, 512, 1024], P('depth', 'tile')
- pressure_new: float32 [256, 512, 1024], P('depth', 'tile')
- image: float32 [4, 512, 1024], P(None, 'tile')
The draws below stay inside these ranges and needn't reach their ends.
All inputs are finite; a program needn't handle non-finite values. No bound on the sum of `solid_flags` on one device may be relied on, other than what follows from the above.
Results may differ from the reference program's by a relative error of at most 0.00005.
Values sent between devices are 32-bit elements; how exact they have to be, the bound alone decides.
A program may use at most 64 MiB of HBM per device.

```python
import jax
import jax.numpy as jnp

NY = 1024
NZ = 256
NX = 512


def place_ends(drawn, rng, smallest, top_value):
    extent = drawn.shape
    index_at = [jax.random.randint(jax.random.fold_in(rng, axis), (), 0, extent[axis]) for axis in range(len(extent))]
    drawn = drawn.at[tuple(index_at)].set(smallest)
    longest = extent.index(max(extent))
    index_at[longest] = (index_at[longest] + 1) % extent[longest]
    return drawn.at[tuple(index_at)].set(top_value)


def level_of(rng, shape, cuts, least, top_value):
    def one(dim, parts):
        steps = jax.random.uniform(jax.random.fold_in(jax.random.fold_in(rng, 6), dim), (parts,), jnp.float32, least / len(cuts), top_value / len(cuts))
        return jnp.repeat(jnp.exp(steps), shape[dim] // parts).reshape((-1,) + (1,) * (len(shape) - dim - 1))

    loudness = one(*cuts[0])
    for cut in cuts[1:]:
        loudness = loudness * one(*cut)
    return loudness


def bell_draw(stream_key, dims, scale, limit, pieces=(), held_as=jnp.bfloat16):
    array = jax.random.normal(stream_key, dims, jnp.float32) * scale
    if len(pieces) > 0:
        array = level_of(stream_key, dims, pieces, -0.22, 0.18) * array
    return jnp.clip(array, min=-limit, max=limit).astype(held_as)


def setup_inputs(seed: int = 0) -> dict:
    key_list = jax.random.split(jax.random.key(seed), 4)
    return {
        "pressure_old": bell_draw(key_list[0], (NZ, NX, NY), 1.0, 6.0, ((0, 32), (1, 8)), jnp.float32),
        "pressure_now": bell_draw(key_list[1], (NZ, NX, NY), 1.0, 6.0, ((0, 32), (1, 8)), jnp.float32),
        "solid_flags": place_ends((jax.random.randint(key_list[2], (NZ, NX, NY), 0, 8) < 1).astype(jnp.int32), jax.random.fold_in(key_list[2], 1), 0, 1),
    }


def advance(previous, current, open_field):
    padded = jnp.pad(current, 1)
    beside = padded[2:, 1:-1, 1:-1] + padded[:-2, 1:-1, 1:-1]
    beside = beside + padded[1:-1, 2:, 1:-1] + padded[1:-1, :-2, 1:-1]
    beside = beside + padded[1:-1, 1:-1, 2:] + padded[1:-1, 1:-1, :-2]
    return open_field * (2.0 * current - previous + 0.3 * (beside - 6.0 * current))


def reference(pressure_old, pressure_now, solid_flags):
    open_field = (1 - solid_flags).astype(jnp.float32)
    pressure_mid = advance(pressure_old, pressure_now, open_field)
    pressure_new = advance(pressure_now, pressure_mid, open_field)
    square = pressure_new * pressure_new
    tau = (4.0 / NZ) * square / (1.0 + square)
    weight = (1.0 - jnp.exp(-tau)) * jnp.exp(-(jnp.cumsum(tau, axis=0) - tau))
    red = jnp.sum(jax.nn.sigmoid(3.0 * pressure_new) * weight, axis=0)
    green = jnp.sum(jnp.exp(-0.5 * square) * weight, axis=0)
    blue = jnp.sum(jax.nn.sigmoid(-3.0 * pressure_new) * weight, axis=0)
    opacity = 1.0 - jnp.exp(-jnp.sum(tau, axis=0))
    return pressure_mid, pressure_new, jnp.stack([red, green, blue, opacity])
```

```python
import functools
import math

import jax
import jax.numpy as jnp
from jax import lax
from jax.experimental import pallas as pl
from jax.experimental.pallas import tpu as pltpu
from jax.sharding import PartitionSpec as P

MESH = pl.DeviceIdType.MESH
LANES = 128
ROWS = 8
SPREAD = 2


def leap(before, field, closed, p, r, l):
    lane = lax.broadcasted_iota(jnp.int32, (ROWS, LANES), 1)
    row = lax.broadcasted_iota(jnp.int32, (ROWS, LANES), 0)

    def tile(dp=0, dr=0, dl=0):
        return field[p + dp, pl.ds(pl.multiple_of(r + dr, ROWS), ROWS), pl.ds(pl.multiple_of(l + dl, LANES), LANES)]

    here = tile()
    west = pltpu.roll(jnp.where(lane == LANES - 1, tile(dl=-LANES), here), 1, 1)
    east = pltpu.roll(jnp.where(lane == 0, tile(dl=LANES), here), LANES - 1, 1)
    north = pltpu.roll(jnp.where(row == ROWS - 1, tile(dr=-ROWS), here), 1, 0)
    south = pltpu.roll(jnp.where(row == 0, tile(dr=ROWS), here), ROWS - 1, 0)
    beside = (tile(dp=-1) + tile(dp=1)) + ((north + south) + (west + east))
    ahead = (0.2 * here - before) + 0.3 * beside
    return jnp.where(closed == 0, ahead, 0.0)


def kernel(
    steps, now_h, old_h, flag_h, mid_h, new_h, image_h,
    now, old, flag, mid, new, part, peer, joint, shares, final, blue,
    load_sem, store_sem, face_send, face_recv, pair_send, pair_recv,
    share_send, share_recv, spread_send, spread_recv, swap_send, swap_recv,
):
    depth_count, tile_count = lax.axis_size("depth"), lax.axis_size("tile")
    d, t = lax.axis_index("depth"), lax.axis_index("tile")
    planes, rows, cols = now_h.shape
    blocks, tiles = rows // ROWS, cols // LANES
    chips = depth_count // 2
    core, chip = lax.rem(d, 2), lax.div(d, 2)
    half = blocks // 2
    d_up, d_down = lax.rem(d + 1, depth_count), lax.rem(d + depth_count - 1, depth_count)
    t_up, t_down = lax.rem(t + 1, tile_count), lax.rem(t + tile_count - 1, tile_count)
    partner = d + 1 - 2 * core
    inner_rows, inner_cols = pl.ds(ROWS, rows), pl.ds(LANES, cols)

    loads = [
        pltpu.make_async_copy(src, dst, load_sem.at[i])
        for i, (src, dst) in enumerate(
            (
                (now_h, now.at[pl.ds(1, planes), inner_rows, inner_cols]),
                (old_h, old),
                (flag_h, flag),
            )
        )
    ]
    for copy in loads:
        copy.start()

    barrier = pltpu.get_barrier_semaphore()
    for who in ((d_up, t), (d_down, t), (d, t_up), (d, t_down)):
        pl.semaphore_signal(barrier, inc=1, device_id=who, device_id_type=MESH)

    def greet(k, carry):
        other = lax.rem(chip + k, chips) * 2 + core
        pl.semaphore_signal(barrier, inc=1, device_id=(other, t), device_id_type=MESH)
        return carry

    lax.fori_loop(1, chips, greet, 0)
    pl.semaphore_wait(barrier, 4 + chips - 1)

    def faces(stage, low, high, first, last, field):
        ends = (
            (low, field.at[planes + 1, inner_rows, inner_cols], (d_down, t)),
            (high, field.at[0, inner_rows, inner_cols], (d_up, t)),
            (first, field.at[pl.ds(1, planes), pl.ds(ROWS + rows, ROWS), inner_cols], (d, t_down)),
            (last, field.at[pl.ds(1, planes), pl.ds(0, ROWS), inner_cols], (d, t_up)),
        )
        return [
            pltpu.make_async_remote_copy(
                src_ref=src,
                dst_ref=dst,
                send_sem=face_send.at[stage, i],
                recv_sem=face_recv.at[stage, i],
                device_id=who,
                device_id_type=MESH,
            )
            for i, (src, dst, who) in enumerate(ends)
        ]

    def clear_edges(field):
        @pl.when(d == 0)
        def _():
            field[0, inner_rows, inner_cols] = jnp.zeros((rows, cols), jnp.float32)

        @pl.when(d == depth_count - 1)
        def _():
            field[planes + 1, inner_rows, inner_cols] = jnp.zeros((rows, cols), jnp.float32)

        @pl.when(t == 0)
        def _():
            field[pl.ds(1, planes), pl.ds(0, ROWS), inner_cols] = jnp.zeros((planes, ROWS, cols), jnp.float32)

        @pl.when(t == tile_count - 1)
        def _():
            field[pl.ds(1, planes), pl.ds(ROWS + rows, ROWS), inner_cols] = jnp.zeros((planes, ROWS, cols), jnp.float32)

    now_faces = faces(
        0,
        now_h.at[0],
        now_h.at[planes - 1],
        now_h.at[:, pl.ds(0, ROWS)],
        now_h.at[:, pl.ds(rows - ROWS, ROWS)],
        now,
    )
    for copy in now_faces:
        copy.start()

    for field in (now, mid):
        for side in (0, LANES + cols):
            field[pl.ds(1, planes), inner_rows, pl.ds(side, LANES)] = jnp.zeros((planes, rows, LANES), jnp.float32)
    for copy in loads:
        copy.wait()

    def over(count, body):
        turns = tiles // SPREAD

        def lap(n, carry):
            i, j = lax.div(n, turns), lax.rem(n, turns)
            for s in range(SPREAD):
                body(i, pl.multiple_of((j * SPREAD + s) * LANES, LANES))
            return carry

        lax.fori_loop(0, count * turns, lap, 0)

    def mid_tile(p, b, l):
        r = pl.multiple_of(b * ROWS, ROWS)
        here = (pl.ds(r, ROWS), pl.ds(l, LANES))
        mid[p + 1, pl.ds(pl.multiple_of(r + ROWS, ROWS), ROWS), pl.ds(pl.multiple_of(l + LANES, LANES), LANES)] = leap(
            old[(p,) + here], now, flag[(p,) + here], p + 1, r + ROWS, l + LANES
        )

    def mid_inner(i, l):
        for p in range(1, planes - 1):
            mid_tile(p, i + 1, l)

    def mid_outer(i, l):
        for p in (0, planes - 1):
            mid_tile(p, i, l)

    def mid_rows(i, l):
        for p in range(1, planes - 1):
            mid_tile(p, i * (blocks - 1), l)

    over(blocks - 2, mid_inner)
    for copy in now_faces:
        copy.wait_recv()
    clear_edges(now)
    over(blocks, mid_outer)
    mid_faces = faces(
        1,
        mid.at[1, inner_rows, inner_cols],
        mid.at[planes, inner_rows, inner_cols],
        mid.at[pl.ds(1, planes), pl.ds(ROWS, ROWS), inner_cols],
        mid.at[pl.ds(1, planes), pl.ds(rows, ROWS), inner_cols],
        mid,
    )
    mid_faces[0].start()
    mid_faces[1].start()
    over(2, mid_rows)
    mid_faces[2].start()
    mid_faces[3].start()
    mid_store = pltpu.make_async_copy(mid.at[pl.ds(1, planes), inner_rows, inner_cols], mid_h, store_sem.at[0])
    mid_store.start()

    rate = steps * math.log2(math.e)

    def new_tile(p, b, l):
        r = pl.multiple_of(b * ROWS, ROWS)
        here = (pl.ds(r, ROWS), pl.ds(l, LANES))
        before = now[p + 1, pl.ds(pl.multiple_of(r + ROWS, ROWS), ROWS), pl.ds(pl.multiple_of(l + LANES, LANES), LANES)]
        value = leap(before, mid, flag[(p,) + here], p + 1, r + ROWS, l + LANES)
        new[(p,) + here] = value
        square = value * value
        thick = square * pltpu.reciprocal(1.0 + square, approx=True)
        return thick, jnp.tanh(1.5 * value), jnp.exp2((-0.5 * math.log2(math.e)) * square)

    def place(b, l):
        return (pl.ds(pl.multiple_of(b * ROWS, ROWS), ROWS), pl.ds(l, LANES))

    def inner(b, l):
        at = place(b, l)
        depth = light = red = green = None
        for p in range(1, planes - 1):
            thick, warm, mild = new_tile(p, b, l)
            if depth is None:
                depth = thick
                after = jnp.exp2(-rate * depth)
                weight = 1.0 - after
                red, green = weight * warm, weight * mild
            else:
                depth = depth + thick
                after = jnp.exp2(-rate * depth)
                weight = light - after
                red, green = red + weight * warm, green + weight * mild
            light = after
        part[(0,) + at], part[(1,) + at], part[(2,) + at] = red, green, depth

    def outer(b, l):
        at = place(b, l)
        depth = part[(2,) + at]
        thick_a, warm_a, mild_a = new_tile(0, b, l)
        thick_b, warm_b, mild_b = new_tile(planes - 1, b, l)
        light_a = jnp.exp2(-rate * thick_a)
        depth_b = thick_a + depth
        light_b = jnp.exp2(-rate * depth_b)
        depth_c = depth_b + thick_b
        light_c = jnp.exp2(-rate * depth_c)
        weight_a, weight_b = 1.0 - light_a, light_b - light_c
        part[(0,) + at] = weight_a * warm_a + light_a * part[(0,) + at] + weight_b * warm_b
        part[(1,) + at] = weight_a * mild_a + light_a * part[(1,) + at] + weight_b * mild_b
        part[(2,) + at] = depth_c

    over(blocks - 2, lambda i, l: inner(i + 1, l))
    for copy in mid_faces:
        copy.wait_recv()
    clear_edges(mid)
    over(2, lambda i, l: inner(i * (blocks - 1), l))

    def pair(i):
        mine = pl.ds(pl.multiple_of(((1 - core) * half + i) * ROWS, ROWS), ROWS)
        theirs = pl.ds(pl.multiple_of(i * ROWS, ROWS), ROWS)
        return pltpu.make_async_remote_copy(
            src_ref=part.at[:, mine],
            dst_ref=peer.at[:, theirs],
            send_sem=pair_send.at[i],
            recv_sem=pair_recv.at[i],
            device_id=(partner, t),
            device_id_type=MESH,
        )

    def give(i, carry):
        over(1, lambda _, l: outer((1 - core) * half + i, l))
        pair(i).start()
        return carry

    lax.fori_loop(0, half, give, 0)

    def share(i, j, who):
        return pltpu.make_async_remote_copy(
            src_ref=joint.at[:, pl.ds(pl.multiple_of(i * ROWS, ROWS), ROWS), pl.ds(pl.multiple_of(j * LANES, LANES), LANES)],
            dst_ref=shares.at[lax.div(i, 2), chip],
            send_sem=share_send.at[lax.div(i, 2), who],
            recv_sem=share_recv.at[lax.div(i, 2), chip],
            device_id=(who * 2 + core, t),
            device_id_type=MESH,
        )

    def join(i, carry):
        over(1, lambda _, l: outer(core * half + i, l))
        pair(i).wait_recv()

        def merge(_, l):
            mine, theirs = place(core * half + i, l), place(i, l)
            first = core == 0
            own = [part[(c,) + mine] for c in range(3)]
            other = [peer[(c,) + theirs] for c in range(3)]
            light = jnp.exp2(-rate * jnp.where(first, own[2], other[2]))
            for c in range(2):
                joint[(c,) + theirs] = jnp.where(first, own[c], other[c]) + light * jnp.where(first, other[c], own[c])
            joint[(2,) + theirs] = own[2] + other[2]

        over(1, merge)

        def send(k, carry):
            j = lax.rem(k + chip, tiles)
            who = lax.rem(i, 2) * tiles + j

            @pl.when(who != chip)
            def _():
                share(i, j, who).start()

            @pl.when(who == chip)
            def _():
                at = place(i, pl.multiple_of(j * LANES, LANES))
                for c in range(3):
                    shares[lax.div(i, 2), chip, c] = joint[(c,) + at]

            return carry

        return lax.fori_loop(0, tiles, send, carry)

    lax.fori_loop(0, half, join, 0)
    new_store = pltpu.make_async_copy(new, new_h, store_sem.at[1])
    new_store.start()

    def spread(s, who):
        i = 2 * s + lax.div(chip, tiles)
        at = final.at[
            :,
            pl.ds(pl.multiple_of((core * half + i) * ROWS, ROWS), ROWS),
            pl.ds(pl.multiple_of(lax.rem(chip, tiles) * LANES, LANES), LANES),
        ]
        return pltpu.make_async_remote_copy(
            src_ref=at,
            dst_ref=at,
            send_sem=spread_send.at[s, who],
            recv_sem=spread_recv.at[s, chip],
            device_id=(who * 2 + core, t),
            device_id_type=MESH,
        )

    def spread_in(s, whose):
        i = 2 * s + lax.div(whose, tiles)
        at = final.at[
            :,
            pl.ds(pl.multiple_of((core * half + i) * ROWS, ROWS), ROWS),
            pl.ds(pl.multiple_of(lax.rem(whose, tiles) * LANES, LANES), LANES),
        ]
        return pltpu.make_async_copy(at, at, spread_recv.at[s, whose])

    def others(body):
        def one(k, carry):
            body(lax.rem(chip + k, chips))
            return carry

        lax.fori_loop(1, chips, one, 0)

    for s in range(2):
        others(lambda who: pltpu.make_async_copy(shares.at[s, who], shares.at[s, who], share_recv.at[s, who]).wait())

        def compose(k, carry):
            red, green, depth = carry
            light = jnp.exp2(-rate * depth)
            return (
                red + light * shares[s, k, 0],
                green + light * shares[s, k, 1],
                depth + shares[s, k, 2],
            )

        zero = jnp.zeros((ROWS, LANES), jnp.float32)
        red, green, depth = lax.fori_loop(0, chips, compose, (zero, zero, zero))
        opacity = 1.0 - jnp.exp2(-rate * depth)
        at = place(
            core * half + 2 * s + lax.div(chip, tiles), pl.multiple_of(lax.rem(chip, tiles) * LANES, LANES)
        )
        final[(0,) + at], final[(1,) + at], final[(2,) + at] = 0.5 * (opacity + red), green, opacity
        others(lambda who: spread(s, who).start())

    def swap(s, whose):
        at = final.at[:, pl.ds(pl.multiple_of((whose * half + 2 * s) * ROWS, ROWS), 2 * ROWS)]
        return pltpu.make_async_remote_copy(
            src_ref=at,
            dst_ref=at,
            send_sem=swap_send.at[s],
            recv_sem=swap_recv.at[s],
            device_id=(partner, t),
            device_id_type=MESH,
        )

    for s in range(2):
        others(lambda who: spread_in(s, who).wait())
        swap(s, core).start()
    for s in range(2):
        swap(s, 1 - core).wait_recv()
    blue[...] = final[2] - final[0]
    image_stores = [
        pltpu.make_async_copy(src, image_h.at[c], store_sem.at[2 + c])
        for c, src in enumerate((final.at[0], final.at[1], blue, final.at[2]))
    ]
    for copy in image_stores:
        copy.start()

    for copy in now_faces + mid_faces:
        copy.wait_send()

    def drain(i, carry):
        pair(i).wait_send()
        return carry

    lax.fori_loop(0, half, drain, 0)
    for s in range(2):
        others(lambda who: pltpu.make_async_copy(shares.at[s, who], shares.at[s, who], share_send.at[s, who]).wait())
        others(lambda who: spread(s, who).wait_send())
        swap(s, core).wait_send()
    mid_store.wait()
    new_store.wait()
    for copy in image_stores:
        copy.wait()


def shards(pressure_old, pressure_now, solid_flags):
    planes, rows, cols = pressure_now.shape
    chips = lax.axis_size("depth") // 2
    half = rows // 2
    any_space = pl.BlockSpec(memory_space=pl.ANY)
    f32 = jnp.float32
    halo = (planes + 2, rows + 2 * ROWS, cols + 2 * LANES)
    return pl.pallas_call(
        functools.partial(kernel, 4.0 / (planes * lax.axis_size("depth"))),
        out_shape=[
            jax.ShapeDtypeStruct(pressure_now.shape, f32),
            jax.ShapeDtypeStruct(pressure_now.shape, f32),
            jax.ShapeDtypeStruct((4, rows, cols), f32),
        ],
        in_specs=[any_space] * 3,
        out_specs=[any_space] * 3,
        scratch_shapes=[
            pltpu.VMEM(halo, f32),
            pltpu.VMEM(pressure_now.shape, f32),
            pltpu.VMEM(pressure_now.shape, jnp.int32),
            pltpu.VMEM(halo, f32),
            pltpu.VMEM(pressure_now.shape, f32),
            pltpu.VMEM((3, rows, cols), f32),
            pltpu.VMEM((3, half, cols), f32),
            pltpu.VMEM((3, half, cols), f32),
            pltpu.VMEM((2, chips, 3, ROWS, LANES), f32),
            pltpu.VMEM((3, rows, cols), f32),
            pltpu.VMEM((rows, cols), f32),
            pltpu.SemaphoreType.DMA((3,)),
            pltpu.SemaphoreType.DMA((6,)),
            pltpu.SemaphoreType.DMA((2, 4)),
            pltpu.SemaphoreType.DMA((2, 4)),
            pltpu.SemaphoreType.DMA((half // ROWS,)),
            pltpu.SemaphoreType.DMA((half // ROWS,)),
            pltpu.SemaphoreType.DMA((2, chips)),
            pltpu.SemaphoreType.DMA((2, chips)),
            pltpu.SemaphoreType.DMA((2, chips)),
            pltpu.SemaphoreType.DMA((2, chips)),
            pltpu.SemaphoreType.DMA((2,)),
            pltpu.SemaphoreType.DMA((2,)),
        ],
        compiler_params=pltpu.CompilerParams(
            collective_id=0, has_side_effects=True, vmem_limit_bytes=48 * 1024 * 1024
        ),
    )(pressure_now, pressure_old, solid_flags)


def solution(mesh):
    return jax.shard_map(
        shards,
        mesh=mesh,
        in_specs=(P("depth", "tile", None), P("depth", "tile", None), P("depth", "tile", None)),
        out_specs=(P("depth", "tile", None), P("depth", "tile", None), P(None, "tile", None)),
        check_vma=False,
    )
```

```python
import functools
import math

import jax
import jax.numpy as jnp
from jax import lax
from jax.experimental import pallas as pl
from jax.experimental.pallas import tpu as pltpu
from jax.sharding import PartitionSpec as P

MESH = pl.DeviceIdType.MESH
LANES = 128
ROWS = 8
SPREAD = 8
PIECES = 4


def leap(before, field, closed, p, r, l):
    lane = lax.broadcasted_iota(jnp.int32, (ROWS, LANES), 1)
    row = lax.broadcasted_iota(jnp.int32, (ROWS, LANES), 0)

    def tile(dp=0, dr=0, dl=0):
        return field[p + dp, pl.ds(pl.multiple_of(r + dr, ROWS), ROWS), pl.ds(pl.multiple_of(l + dl, LANES), LANES)]

    here = tile()
    west = pltpu.roll(jnp.where(lane == LANES - 1, tile(dl=-LANES), here), 1, 1)
    east = pltpu.roll(jnp.where(lane == 0, tile(dl=LANES), here), LANES - 1, 1)
    north = pltpu.roll(jnp.where(row == ROWS - 1, tile(dr=-ROWS), here), 1, 0)
    south = pltpu.roll(jnp.where(row == 0, tile(dr=ROWS), here), ROWS - 1, 0)
    beside = (tile(dp=-1) + tile(dp=1)) + ((north + south) + (west + east))
    ahead = (0.2 * here - before) + 0.3 * beside
    return jnp.where(closed == 0, ahead, 0.0)


def kernel(
    steps, now_h, old_h, flag_h, mid_h, new_h, image_h,
    now, old, flag, mid, new, part, peer, joint, shares, final, blue,
    load_sem, store_sem, face_send, face_recv, edge_send, edge_recv, pair_send, pair_recv,
    share_send, share_recv, spread_send, spread_recv, swap_send, swap_recv,
):
    depth_count, tile_count = lax.axis_size("depth"), lax.axis_size("tile")
    d, t = lax.axis_index("depth"), lax.axis_index("tile")
    planes, rows, cols = now_h.shape
    blocks, tiles = rows // ROWS, cols // LANES
    chips = depth_count // 2
    core, chip = lax.rem(d, 2), lax.div(d, 2)
    piece = rows // PIECES
    d_up, d_down = lax.rem(d + 1, depth_count), lax.rem(d + depth_count - 1, depth_count)
    t_up, t_down = lax.rem(t + 1, tile_count), lax.rem(t + tile_count - 1, tile_count)
    has_d_up, has_d_down = d < depth_count - 1, d > 0
    has_t_up, has_t_down = t < tile_count - 1, t > 0
    partner = d + 1 - 2 * core
    inner_rows, inner_cols = pl.ds(ROWS, rows), pl.ds(LANES, cols)
    near = (
        (has_d_up, (d_up, t)),
        (has_d_down, (d_down, t)),
        (has_t_up, (d, t_up)),
        (has_t_down, (d, t_down)),
    )

    barrier = pltpu.get_barrier_semaphore()
    for there, who in near:

        @pl.when(there)
        def _():
            pl.semaphore_signal(barrier, inc=1, device_id=who, device_id_type=MESH)

    def greet(k, carry):
        other = lax.rem(chip + k, chips) * 2 + core
        pl.semaphore_signal(barrier, inc=1, device_id=(other, t), device_id_type=MESH)
        return carry

    lax.fori_loop(1, chips, greet, 0)

    loads = [
        pltpu.make_async_copy(src, dst, load_sem.at[i])
        for i, (src, dst) in enumerate(
            (
                (now_h, now.at[pl.ds(1, planes), inner_rows, inner_cols]),
                (old_h, old),
                (flag_h, flag),
            )
        )
    ]
    for copy in loads:
        copy.start()
    for field in (now, mid):
        for side in (0, LANES + cols):
            field[pl.ds(1, planes), inner_rows, pl.ds(side, LANES)] = jnp.zeros((planes, rows, LANES), jnp.float32)

        @pl.when(jnp.logical_not(has_d_down))
        def _():
            field[0, inner_rows, inner_cols] = jnp.zeros((rows, cols), jnp.float32)

        @pl.when(jnp.logical_not(has_d_up))
        def _():
            field[planes + 1, inner_rows, inner_cols] = jnp.zeros((rows, cols), jnp.float32)

        @pl.when(jnp.logical_not(has_t_down))
        def _():
            field[pl.ds(1, planes), pl.ds(0, ROWS), inner_cols] = jnp.zeros((planes, ROWS, cols), jnp.float32)

        @pl.when(jnp.logical_not(has_t_up))
        def _():
            field[pl.ds(1, planes), pl.ds(ROWS + rows, ROWS), inner_cols] = jnp.zeros((planes, ROWS, cols), jnp.float32)

    count = chips - 1
    for left in (d, depth_count - 1 - d, t, tile_count - 1 - t):
        count = count + jnp.minimum(left, 1)
    pl.semaphore_wait(barrier, count)

    def depth_face(stage, way, q):
        plane = (planes - 1) * way
        if stage == 0:
            src, field = now_h.at[plane, pl.ds(q * piece, piece)], now
        else:
            src, field = mid.at[plane + 1, pl.ds(ROWS + q * piece, piece), inner_cols], mid
        return pltpu.make_async_remote_copy(
            src_ref=src,
            dst_ref=field.at[(planes + 1) * (1 - way), pl.ds(ROWS + q * piece, piece), inner_cols],
            send_sem=face_send.at[stage, way, q],
            recv_sem=face_recv.at[stage, way, q],
            device_id=((d_down, d_up)[way], t),
            device_id_type=MESH,
        )

    def tile_face(stage, way):
        row = (rows - 1) * way
        if stage == 0:
            src, field = now_h.at[:, pl.ds(row, 1)], now
        else:
            src, field = mid.at[pl.ds(1, planes), pl.ds(ROWS + row, 1), inner_cols], mid
        return pltpu.make_async_remote_copy(
            src_ref=src,
            dst_ref=field.at[pl.ds(1, planes), pl.ds(ROWS + rows if way == 0 else ROWS - 1, 1), inner_cols],
            send_sem=edge_send.at[stage, way],
            recv_sem=edge_recv.at[stage, way],
            device_id=(d, (t_down, t_up)[way]),
            device_id_type=MESH,
        )

    d_to, t_to = (has_d_down, has_d_up), (has_t_down, has_t_up)
    d_from, t_from = d_to[::-1], t_to[::-1]

    def start_depth(stage, q):
        for way in range(2):
            pl.when(d_to[way])(lambda: depth_face(stage, way, q).start())

    def start_tile(stage, way):
        pl.when(t_to[way])(lambda: tile_face(stage, way).start())

    def await_depth(stage, q):
        for way in range(2):
            pl.when(d_from[way])(lambda: depth_face(stage, way, q).wait_recv())

    def await_tile(stage, way):
        pl.when(t_from[way])(lambda: tile_face(stage, way).wait_recv())

    for way in range(2):
        start_tile(0, way)
    for q in range(PIECES):
        start_depth(0, q)

    for copy in loads:
        copy.wait()

    def over(count, body):
        turns = tiles // SPREAD

        def lap(n, carry):
            i, j = lax.div(n, turns), lax.rem(n, turns)
            for s in range(SPREAD):
                body(i, pl.multiple_of((j * SPREAD + s) * LANES, LANES))
            return carry

        lax.fori_loop(0, count * turns, lap, 0)

    def mid_tile(p, b, l):
        r = pl.multiple_of(b * ROWS, ROWS)
        here = (pl.ds(r, ROWS), pl.ds(l, LANES))
        mid[p + 1, pl.ds(pl.multiple_of(r + ROWS, ROWS), ROWS), pl.ds(pl.multiple_of(l + LANES, LANES), LANES)] = leap(
            old[(p,) + here], now, flag[(p,) + here], p + 1, r + ROWS, l + LANES
        )

    def mid_inner(b, l):
        for p in range(1, planes - 1):
            mid_tile(p, b, l)

    def mid_outer(b, l):
        for p in (0, planes - 1):
            mid_tile(p, b, l)

    over(blocks - 2, lambda i, l: mid_inner(i + 1, l))
    for way in range(2):
        await_tile(0, way)
    over(2, lambda i, l: mid_inner(i * (blocks - 1), l))
    per = blocks // PIECES
    for q in range(PIECES):
        await_depth(0, q)
        over(per, lambda i, l: mid_outer(q * per + i, l))
        start_depth(1, q)
        if q == 0:
            start_tile(1, 0)
    start_tile(1, 1)
    mid_store = pltpu.make_async_copy(mid.at[pl.ds(1, planes), inner_rows, inner_cols], mid_h, store_sem.at[0])
    mid_store.start()

    rate = steps * math.log2(math.e)

    def new_tile(p, b, l):
        r = pl.multiple_of(b * ROWS, ROWS)
        here = (pl.ds(r, ROWS), pl.ds(l, LANES))
        before = now[p + 1, pl.ds(pl.multiple_of(r + ROWS, ROWS), ROWS), pl.ds(pl.multiple_of(l + LANES, LANES), LANES)]
        value = leap(before, mid, flag[(p,) + here], p + 1, r + ROWS, l + LANES)
        new[(p,) + here] = value
        square = value * value
        thick = square * pltpu.reciprocal(1.0 + square, approx=True)
        return thick, jnp.tanh(1.5 * value), jnp.exp2((-0.5 * math.log2(math.e)) * square)

    def place(b, l):
        return (pl.ds(pl.multiple_of(b * ROWS, ROWS), ROWS), pl.ds(l, LANES))

    def inner(b, l):
        at = place(b, l)
        depth = light = red = green = None
        for p in range(1, planes - 1):
            thick, warm, mild = new_tile(p, b, l)
            if depth is None:
                depth = thick
                after = jnp.exp2(-rate * depth)
                weight = 1.0 - after
                red, green = weight * warm, weight * mild
            else:
                depth = depth + thick
                after = jnp.exp2(-rate * depth)
                weight = light - after
                red, green = red + weight * warm, green + weight * mild
            light = after
        part[(0,) + at], part[(1,) + at], part[(2,) + at] = red, green, depth

    def outer(b, l):
        at = place(b, l)
        depth = part[(2,) + at]
        thick_a, warm_a, mild_a = new_tile(0, b, l)
        thick_b, warm_b, mild_b = new_tile(planes - 1, b, l)
        light_a = jnp.exp2(-rate * thick_a)
        depth_b = thick_a + depth
        light_b = jnp.exp2(-rate * depth_b)
        depth_c = depth_b + thick_b
        light_c = jnp.exp2(-rate * depth_c)
        weight_a, weight_b = 1.0 - light_a, light_b - light_c
        part[(0,) + at] = weight_a * warm_a + light_a * part[(0,) + at] + weight_b * warm_b
        part[(1,) + at] = weight_a * mild_a + light_a * part[(1,) + at] + weight_b * mild_b
        part[(2,) + at] = depth_c

    def joined(s, whose):
        return 4 * s + 2 * whose

    def pair(s):
        return pltpu.make_async_remote_copy(
            src_ref=part.at[:, pl.ds(pl.multiple_of(joined(s, 1 - core) * ROWS, ROWS), 2 * ROWS)],
            dst_ref=peer.at[s],
            send_sem=pair_send.at[s],
            recv_sem=pair_recv.at[s],
            device_id=(partner, t),
            device_id_type=MESH,
        )

    def share(s, n, who):
        i, j = lax.div(n, tiles), lax.rem(n, tiles)
        return pltpu.make_async_remote_copy(
            src_ref=joint.at[s, :, pl.ds(pl.multiple_of(i * ROWS, ROWS), ROWS), pl.ds(pl.multiple_of(j * LANES, LANES), LANES)],
            dst_ref=shares.at[s, chip],
            send_sem=share_send.at[s, who],
            recv_sem=share_recv.at[s, chip],
            device_id=(who * 2 + core, t),
            device_id_type=MESH,
        )

    def others(body):
        def one(k, carry):
            body(lax.rem(chip + k, chips))
            return carry

        lax.fori_loop(1, chips, one, 0)

    over(blocks - 2, lambda i, l: inner(i + 1, l))
    for s in range(2):
        await_tile(1, 1 - s)
        over(1, lambda _, l: inner(s * (blocks - 1), l))
        for q in range(s * PIECES // 2, (s + 1) * PIECES // 2):
            await_depth(1, q)
        over(2, lambda i, l: outer(joined(s, 1 - core) + i, l))
        pair(s).start()
        over(2, lambda i, l: outer(joined(s, core) + i, l))
        if s == 1:
            new_store = pltpu.make_async_copy(new, new_h, store_sem.at[1])
            new_store.start()
        pair(s).wait_recv()

        def merge(i, l):
            mine, theirs = place(joined(s, core) + i, l), place(i, l)
            first = core == 0
            own = [part[(c,) + mine] for c in range(3)]
            other = [peer[(s, c) + theirs] for c in range(3)]
            light = jnp.exp2(-rate * jnp.where(first, own[2], other[2]))
            for c in range(2):
                joint[(s, c) + theirs] = jnp.where(first, own[c], other[c]) + light * jnp.where(first, other[c], own[c])
            joint[(s, 2) + theirs] = own[2] + other[2]

        over(2, merge)
        others(lambda who: share(s, who, who).start())
        own_tile = place(lax.div(chip, tiles), pl.multiple_of(lax.rem(chip, tiles) * LANES, LANES))
        for c in range(3):
            shares[s, chip, c] = joint[(s, c) + own_tile]

    def region(s, whose):
        at = place(
            joined(s, core) + lax.div(whose, tiles), pl.multiple_of(lax.rem(whose, tiles) * LANES, LANES)
        )
        return final.at[(slice(None),) + at]

    def spread(s, who):
        return pltpu.make_async_remote_copy(
            src_ref=region(s, chip),
            dst_ref=region(s, chip),
            send_sem=spread_send.at[s, who],
            recv_sem=spread_recv.at[s, chip],
            device_id=(who * 2 + core, t),
            device_id_type=MESH,
        )

    def swap(s, whose):
        at = final.at[:, pl.ds(pl.multiple_of(joined(s, whose) * ROWS, ROWS), 2 * ROWS)]
        return pltpu.make_async_remote_copy(
            src_ref=at,
            dst_ref=at,
            send_sem=swap_send.at[s],
            recv_sem=swap_recv.at[s],
            device_id=(partner, t),
            device_id_type=MESH,
        )

    for s in range(2):
        others(lambda who: pltpu.make_async_copy(shares.at[s, who], shares.at[s, who], share_recv.at[s, who]).wait())

        def compose(k, carry):
            red, green, depth = carry
            light = jnp.exp2(-rate * depth)
            return (
                red + light * shares[s, k, 0],
                green + light * shares[s, k, 1],
                depth + shares[s, k, 2],
            )

        zero = jnp.zeros((ROWS, LANES), jnp.float32)
        red, green, depth = lax.fori_loop(0, chips, compose, (zero, zero, zero))
        opacity = 1.0 - jnp.exp2(-rate * depth)
        at = place(
            joined(s, core) + lax.div(chip, tiles), pl.multiple_of(lax.rem(chip, tiles) * LANES, LANES)
        )
        final[(0,) + at], final[(1,) + at], final[(2,) + at] = 0.5 * (opacity + red), green, opacity
        others(lambda who: spread(s, who).start())

    image_stores = []
    for s in range(2):
        others(lambda who: pltpu.make_async_copy(region(s, who), region(s, who), spread_recv.at[s, who]).wait())
        swap(s, core).start()
    for s in range(2):
        swap(s, 1 - core).wait_recv()
        half = pl.ds(s * rows // 2, rows // 2)
        blue[half] = final[2, half] - final[0, half]
        for c, src in enumerate((final.at[0, half], final.at[1, half], blue.at[half], final.at[2, half])):
            copy = pltpu.make_async_copy(src, image_h.at[c, half], store_sem.at[2 + 4 * s + c])
            copy.start()
            image_stores.append(copy)

    for stage in range(2):
        for way in range(2):
            for q in range(PIECES):
                pl.when(d_to[way])(lambda: depth_face(stage, way, q).wait_send())
            pl.when(t_to[way])(lambda: tile_face(stage, way).wait_send())
    for s in range(2):
        pair(s).wait_send()
        others(lambda who: share(s, who, who).wait_send())
        others(lambda who: spread(s, who).wait_send())
        swap(s, core).wait_send()
    mid_store.wait()
    new_store.wait()
    for copy in image_stores:
        copy.wait()


def shards(pressure_old, pressure_now, solid_flags):
    planes, rows, cols = pressure_now.shape
    chips = lax.axis_size("depth") // 2
    any_space = pl.BlockSpec(memory_space=pl.ANY)
    f32 = jnp.float32
    halo = (planes + 2, rows + 2 * ROWS, cols + 2 * LANES)
    return pl.pallas_call(
        functools.partial(kernel, 4.0 / (planes * lax.axis_size("depth"))),
        out_shape=[
            jax.ShapeDtypeStruct(pressure_now.shape, f32),
            jax.ShapeDtypeStruct(pressure_now.shape, f32),
            jax.ShapeDtypeStruct((4, rows, cols), f32),
        ],
        in_specs=[any_space] * 3,
        out_specs=[any_space] * 3,
        scratch_shapes=[
            pltpu.VMEM(halo, f32),
            pltpu.VMEM(pressure_now.shape, f32),
            pltpu.VMEM(pressure_now.shape, jnp.int32),
            pltpu.VMEM(halo, f32),
            pltpu.VMEM(pressure_now.shape, f32),
            pltpu.VMEM((3, rows, cols), f32),
            pltpu.VMEM((2, 3, 2 * ROWS, cols), f32),
            pltpu.VMEM((2, 3, 2 * ROWS, cols), f32),
            pltpu.VMEM((2, chips, 3, ROWS, LANES), f32),
            pltpu.VMEM((3, rows, cols), f32),
            pltpu.VMEM((rows, cols), f32),
            pltpu.SemaphoreType.DMA((3,)),
            pltpu.SemaphoreType.DMA((10,)),
            pltpu.SemaphoreType.DMA((2, 2, PIECES)),
            pltpu.SemaphoreType.DMA((2, 2, PIECES)),
            pltpu.SemaphoreType.DMA((2, 2)),
            pltpu.SemaphoreType.DMA((2, 2)),
            pltpu.SemaphoreType.DMA((2,)),
            pltpu.SemaphoreType.DMA((2,)),
            pltpu.SemaphoreType.DMA((2, chips)),
            pltpu.SemaphoreType.DMA((2, chips)),
            pltpu.SemaphoreType.DMA((2, chips)),
            pltpu.SemaphoreType.DMA((2, chips)),
            pltpu.SemaphoreType.DMA((2,)),
            pltpu.SemaphoreType.DMA((2,)),
        ],
        compiler_params=pltpu.CompilerParams(
            collective_id=0, has_side_effects=True, vmem_limit_bytes=48 * 1024 * 1024
        ),
    )(pressure_now, pressure_old, solid_flags)


def solution(mesh):
    return jax.shard_map(
        shards,
        mesh=mesh,
        in_specs=(P("depth", "tile", None), P("depth", "tile", None), P("depth", "tile", None)),
        out_specs=(P("depth", "tile", None), P("depth", "tile", None), P(None, "tile", None)),
        check_vma=False,
    )
```

```python
import functools
import math

import jax
import jax.numpy as jnp
from jax import lax
from jax.experimental import pallas as pl
from jax.experimental.pallas import tpu as pltpu
from jax.sharding import PartitionSpec as P

MESH = pl.DeviceIdType.MESH
LANES = 128
ROWS = 8
SPREAD = 8
PIECES = 4


def leap(before, field, closed, p, r, l):
    lane = lax.broadcasted_iota(jnp.int32, (ROWS, LANES), 1)
    row = lax.broadcasted_iota(jnp.int32, (ROWS, LANES), 0)

    def tile(dp=0, dr=0, dl=0):
        return field[p + dp, pl.ds(pl.multiple_of(r + dr, ROWS), ROWS), pl.ds(pl.multiple_of(l + dl, LANES), LANES)]

    here = tile()
    west = pltpu.roll(jnp.where(lane == LANES - 1, tile(dl=-LANES), here), 1, 1)
    east = pltpu.roll(jnp.where(lane == 0, tile(dl=LANES), here), LANES - 1, 1)
    north = pltpu.roll(jnp.where(row == ROWS - 1, tile(dr=-ROWS), here), 1, 0)
    south = pltpu.roll(jnp.where(row == 0, tile(dr=ROWS), here), ROWS - 1, 0)
    beside = (tile(dp=-1) + tile(dp=1)) + ((north + south) + (west + east))
    ahead = (0.2 * here - before) + 0.3 * beside
    return jnp.where(closed == 0, ahead, 0.0)


def kernel(
    steps, now_h, old_h, flag_h, mid_out, new, image,
    now, old, flag, mid, part, peer, joint, shares, final,
    load_sem, store_sem, face_send, face_recv, edge_send, edge_recv, pair_send, pair_recv,
    share_send, share_recv, spread_send, spread_recv, swap_send, swap_recv,
):
    depth_count, tile_count = lax.axis_size("depth"), lax.axis_size("tile")
    d, t = lax.axis_index("depth"), lax.axis_index("tile")
    planes, rows, cols = now_h.shape
    blocks, tiles = rows // ROWS, cols // LANES
    chips = depth_count // 2
    core, chip = lax.rem(d, 2), lax.div(d, 2)
    width = math.isqrt(chips)
    piece = rows // PIECES
    d_up, d_down = lax.rem(d + 1, depth_count), lax.rem(d + depth_count - 1, depth_count)
    t_up, t_down = lax.rem(t + 1, tile_count), lax.rem(t + tile_count - 1, tile_count)
    has_d_up, has_d_down = d < depth_count - 1, d > 0
    has_t_up, has_t_down = t < tile_count - 1, t > 0
    partner = d + 1 - 2 * core
    inner_rows, inner_cols = pl.ds(ROWS, rows), pl.ds(LANES, cols)
    near = (
        (has_d_up, (d_up, t)),
        (has_d_down, (d_down, t)),
        (has_t_up, (d, t_up)),
        (has_t_down, (d, t_down)),
    )

    barrier = pltpu.get_barrier_semaphore()
    for there, who in near:

        @pl.when(there)
        def _():
            pl.semaphore_signal(barrier, inc=1, device_id=who, device_id_type=MESH)

    def load(q):
        at = pl.ds(q * piece, piece)
        return [
            pltpu.make_async_copy(src.at[:, at], dst, load_sem.at[q])
            for src, dst in (
                (now_h, now.at[pl.ds(1, planes), pl.ds(ROWS + q * piece, piece), inner_cols]),
                (old_h, old.at[:, at]),
                (flag_h, flag.at[:, at]),
            )
        ]

    def await_load(q):
        three = old.at[:, pl.ds(0, 3 * piece)]
        pltpu.make_async_copy(three, three, load_sem.at[q]).wait()

    for q in range(PIECES):
        for copy in load(q):
            copy.start()

    for k in range(1, chips):
        other = lax.rem(chip + k, chips) * 2 + core
        pl.semaphore_signal(barrier, inc=1, device_id=(other, t), device_id_type=MESH)

    count = chips - 1
    for left in (d, depth_count - 1 - d, t, tile_count - 1 - t):
        count = count + jnp.minimum(left, 1)
    pl.semaphore_wait(barrier, count)

    def depth_face(stage, way, q):
        plane = (planes - 1) * way
        if stage == 0:
            src, field = now_h.at[plane, pl.ds(q * piece, piece)], now
        else:
            src, field = mid.at[plane + 1, pl.ds(ROWS + q * piece, piece), inner_cols], mid
        return pltpu.make_async_remote_copy(
            src_ref=src,
            dst_ref=field.at[(planes + 1) * (1 - way), pl.ds(ROWS + q * piece, piece), inner_cols],
            send_sem=face_send.at[way],
            recv_sem=face_recv.at[stage, way, q],
            device_id=((d_down, d_up)[way], t),
            device_id_type=MESH,
        )

    def tile_face(stage, way):
        row = (rows - 1) * way
        if stage == 0:
            src, field = now_h.at[:, pl.ds(row, 1)], now
        else:
            src, field = mid.at[pl.ds(1, planes), pl.ds(ROWS + row, 1), inner_cols], mid
        return pltpu.make_async_remote_copy(
            src_ref=src,
            dst_ref=field.at[pl.ds(1, planes), pl.ds(ROWS + rows if way == 0 else ROWS - 1, 1), inner_cols],
            send_sem=edge_send.at[way],
            recv_sem=edge_recv.at[stage, way],
            device_id=(d, (t_down, t_up)[way]),
            device_id_type=MESH,
        )

    d_to, t_to = (has_d_down, has_d_up), (has_t_down, has_t_up)
    d_from, t_from = d_to[::-1], t_to[::-1]

    def start_depth(stage, q):
        for way in range(2):
            pl.when(d_to[way])(lambda: depth_face(stage, way, q).start())

    def start_tile(stage, way):
        pl.when(t_to[way])(lambda: tile_face(stage, way).start())

    def await_depth(stage, q):
        for way in range(2):
            pl.when(d_from[way])(lambda: depth_face(stage, way, q).wait_recv())

    def await_tile(stage, way):
        pl.when(t_from[way])(lambda: tile_face(stage, way).wait_recv())

    for way in range(2):
        start_tile(0, way)
    for q in range(PIECES):
        start_depth(0, q)

    for field in (now, mid):
        for side in (0, LANES + cols):
            field[pl.ds(1, planes), inner_rows, pl.ds(side, LANES)] = jnp.zeros((planes, rows, LANES), jnp.float32)

        @pl.when(jnp.logical_not(has_d_down))
        def _():
            field[0, inner_rows, inner_cols] = jnp.zeros((rows, cols), jnp.float32)

        @pl.when(jnp.logical_not(has_d_up))
        def _():
            field[planes + 1, inner_rows, inner_cols] = jnp.zeros((rows, cols), jnp.float32)

        @pl.when(jnp.logical_not(has_t_down))
        def _():
            field[pl.ds(1, planes), pl.ds(0, ROWS), inner_cols] = jnp.zeros((planes, ROWS, cols), jnp.float32)

        @pl.when(jnp.logical_not(has_t_up))
        def _():
            field[pl.ds(1, planes), pl.ds(ROWS + rows, ROWS), inner_cols] = jnp.zeros((planes, ROWS, cols), jnp.float32)

    def over(count, body):
        turns = tiles // SPREAD

        def lap(n, carry):
            i, j = lax.div(n, turns), lax.rem(n, turns)
            for s in range(SPREAD):
                body(i, pl.multiple_of((j * SPREAD + s) * LANES, LANES))
            return carry

        lax.fori_loop(0, count * turns, lap, 0)

    def mid_tile(p, b, l):
        r = pl.multiple_of(b * ROWS, ROWS)
        here = (pl.ds(r, ROWS), pl.ds(l, LANES))
        mid[p + 1, pl.ds(pl.multiple_of(r + ROWS, ROWS), ROWS), pl.ds(pl.multiple_of(l + LANES, LANES), LANES)] = leap(
            old[(p,) + here], now, flag[(p,) + here], p + 1, r + ROWS, l + LANES
        )

    def mid_inner(b, l):
        for p in range(1, planes - 1):
            mid_tile(p, b, l)

    def mid_outer(b, l):
        for p in (0, planes - 1):
            mid_tile(p, b, l)

    rate = steps * math.log2(math.e)

    def new_tile(p, b, l):
        r = pl.multiple_of(b * ROWS, ROWS)
        here = (pl.ds(r, ROWS), pl.ds(l, LANES))
        before = now[p + 1, pl.ds(pl.multiple_of(r + ROWS, ROWS), ROWS), pl.ds(pl.multiple_of(l + LANES, LANES), LANES)]
        value = leap(before, mid, flag[(p,) + here], p + 1, r + ROWS, l + LANES)
        new[(p,) + here] = value
        square = value * value
        thick = square * pltpu.reciprocal(1.0 + square, approx=True)
        return thick, jnp.tanh(1.5 * value), jnp.exp2((-0.5 * math.log2(math.e)) * square)

    def place(b, l):
        return (pl.ds(pl.multiple_of(b * ROWS, ROWS), ROWS), pl.ds(l, LANES))

    def inner(b, l):
        at = place(b, l)
        depth = light = red = green = None
        for p in range(1, planes - 1):
            thick, warm, mild = new_tile(p, b, l)
            if depth is None:
                depth = thick
                after = jnp.exp2(-rate * depth)
                weight = 1.0 - after
                red, green = weight * warm, weight * mild
            else:
                depth = depth + thick
                after = jnp.exp2(-rate * depth)
                weight = light - after
                red, green = red + weight * warm, green + weight * mild
            light = after
        part[(0,) + at], part[(1,) + at], part[(2,) + at] = red, green, depth

    def outer(b, l):
        at = place(b, l)
        depth = part[(2,) + at]
        thick_a, warm_a, mild_a = new_tile(0, b, l)
        thick_b, warm_b, mild_b = new_tile(planes - 1, b, l)
        light_a = jnp.exp2(-rate * thick_a)
        depth_b = thick_a + depth
        light_b = jnp.exp2(-rate * depth_b)
        depth_c = depth_b + thick_b
        light_c = jnp.exp2(-rate * depth_c)
        weight_a, weight_b = 1.0 - light_a, light_b - light_c
        part[(0,) + at] = weight_a * warm_a + light_a * part[(0,) + at] + weight_b * warm_b
        part[(1,) + at] = weight_a * mild_a + light_a * part[(1,) + at] + weight_b * mild_b
        part[(2,) + at] = depth_c

    per = blocks // PIECES
    await_load(0)
    for q in range(1, PIECES):
        await_load(q)
        over(per, lambda i, l: mid_inner((q - 1) * per + 1 + i, l))
    for way in range(2):
        await_tile(0, way)
    over(2, lambda i, l: mid_inner(i * (blocks - 1), l))
    for q in range(PIECES):
        await_depth(0, q)
        over(per, lambda i, l: mid_outer(q * per + i, l))
        start_depth(1, q)
        if q == 0:
            start_tile(1, 0)
        else:
            if q == PIECES - 1:
                start_tile(1, 1)
            over(per, lambda i, l: inner((q - 1) * per + 1 + i, l))
    mid_store = pltpu.make_async_copy(mid.at[pl.ds(1, planes), inner_rows, inner_cols], mid_out, store_sem)
    mid_store.start()

    x, y = lax.div(chip, width), lax.rem(chip, width)
    own_tile = x * 2 + lax.div(y, 2)

    def owner(s, j):
        ox = lax.div(j, 2)
        return ox * width + 2 * lax.rem(j, 2) + lax.rem(ox + s, 2)

    def owns(s):
        return lax.rem(x + y + s, 2) == 0

    def block_rows(s, whose):
        return pl.ds(pl.multiple_of((2 * s + whose) * ROWS, ROWS), ROWS)

    def tile_cols(j):
        return pl.ds(pl.multiple_of(j * LANES, LANES), LANES)

    def pair(s):
        return pltpu.make_async_remote_copy(
            src_ref=part.at[:, block_rows(s, 1 - core)],
            dst_ref=peer.at[s],
            send_sem=pair_send,
            recv_sem=pair_recv.at[s],
            device_id=(partner, t),
            device_id_type=MESH,
        )

    def share(s, j):
        return pltpu.make_async_remote_copy(
            src_ref=joint.at[s, :, :, tile_cols(j)],
            dst_ref=shares.at[s, chip],
            send_sem=share_send,
            recv_sem=share_recv.at[s],
            device_id=(owner(s, j) * 2 + core, t),
            device_id_type=MESH,
        )

    def region(s, j):
        return final.at[:, block_rows(s, core), tile_cols(j)]

    def spread(s, who):
        return pltpu.make_async_remote_copy(
            src_ref=region(s, own_tile),
            dst_ref=region(s, own_tile),
            send_sem=spread_send,
            recv_sem=spread_recv.at[s],
            device_id=(who * 2 + core, t),
            device_id_type=MESH,
        )

    def swap(s, whose):
        at = final.at[:, block_rows(s, whose)]
        return pltpu.make_async_remote_copy(
            src_ref=at,
            dst_ref=at,
            send_sem=swap_send,
            recv_sem=swap_recv.at[s],
            device_id=(partner, t),
            device_id_type=MESH,
        )

    def await_tiles(sem, count):
        some = shares.at[pl.ds(0, 2), pl.ds(0, count // 2)] if count > chips else shares.at[0, pl.ds(0, count)]
        pltpu.make_async_copy(some, some, sem).wait()

    def shade(s):
        if s == 0:
            await_tile(1, 1)
            over(1, lambda _, l: inner(0, l))
        if s == PIECES - 1:
            await_tile(1, 0)
            over(1, lambda _, l: inner(blocks - 1, l))
        await_depth(1, s)
        over(1, lambda _, l: outer(2 * s + 1 - core, l))
        pair(s).start()
        over(1, lambda _, l: outer(2 * s + core, l))

    def join(s):
        pair(s).wait_recv()

        def merge(_, l):
            mine, first = (block_rows(s, core), pl.ds(l, LANES)), core == 0
            theirs = (slice(None), pl.ds(l, LANES))
            own = [part[(c,) + mine] for c in range(3)]
            other = [peer[(s, c) + theirs] for c in range(3)]
            light = jnp.exp2(-rate * jnp.where(first, own[2], other[2]))
            for c in range(2):
                joint[(s, c) + theirs] = jnp.where(first, own[c], other[c]) + light * jnp.where(first, other[c], own[c])
            joint[(s, 2) + theirs] = own[2] + other[2]

        over(1, merge)
        for k in range(tiles):
            j = lax.rem(chip + k, tiles)
            pl.when(owner(s, j) != chip)(lambda: share(s, j).start())

        @pl.when(owns(s))
        def _():
            for c in range(3):
                shares[s, chip, c] = joint[s, c, :, tile_cols(own_tile)]

    def compose(s):
        @pl.when(owns(s))
        def _():
            await_tiles(share_recv.at[s], chips - 1)
            red, green, depth = (shares[s, 0, c] for c in range(3))
            for k in range(1, chips):
                light = jnp.exp2(-rate * depth)
                red, green = red + light * shares[s, k, 0], green + light * shares[s, k, 1]
                depth = depth + shares[s, k, 2]
            opacity = 1.0 - jnp.exp2(-rate * depth)
            for c, value in enumerate((0.5 * (opacity + red), green, opacity)):
                final[c, block_rows(s, core), tile_cols(own_tile)] = value
            for k in range(1, chips):
                spread(s, lax.rem(chip + k, chips)).start()

    def gather(s):
        pl.when(owns(s))(lambda: await_tiles(spread_recv.at[s], tiles - 1))
        pl.when(jnp.logical_not(owns(s)))(lambda: await_tiles(spread_recv.at[s], tiles))
        swap(s, core).start()

    def finish(s):
        swap(s, 1 - core).wait_recv()
        at = pl.ds(2 * s * ROWS, 2 * ROWS)
        red, green, opacity = (final[c, at] for c in range(3))
        for c, value in enumerate((red, green, opacity - red, opacity)):
            image[c, at] = value

    shade(0)
    for s in range(1, PIECES):
        shade(s)
        join(s - 1)
    join(PIECES - 1)
    for s in range(PIECES):
        compose(s)
    for s in range(PIECES):
        gather(s)
        if s > 0:
            finish(s - 1)
    finish(PIECES - 1)

    def sent(like, sem):
        pltpu.make_async_copy(like, like, sem).wait()

    for way in range(2):
        pl.when(d_to[way])(lambda: sent(now.at[pl.ds(0, 2), inner_rows, inner_cols], face_send.at[way]))
        pl.when(t_to[way])(lambda: sent(old.at[0, pl.ds(0, 2 * planes)], edge_send.at[way]))
    sent(peer, pair_send)
    await_tiles(share_send, PIECES * tiles - 2)
    await_tiles(spread_send, 2 * (chips - 1))
    sent(peer, swap_send)
    mid_store.wait()


def shards(pressure_old, pressure_now, solid_flags):
    planes, rows, cols = pressure_now.shape
    chips = lax.axis_size("depth") // 2
    any_space = pl.BlockSpec(memory_space=pl.ANY)
    f32 = jnp.float32
    halo = (planes + 2, rows + 2 * ROWS, cols + 2 * LANES)
    return pl.pallas_call(
        functools.partial(kernel, 4.0 / (planes * lax.axis_size("depth"))),
        out_shape=[
            jax.ShapeDtypeStruct(pressure_now.shape, f32),
            jax.ShapeDtypeStruct(pressure_now.shape, f32),
            jax.ShapeDtypeStruct((4, rows, cols), f32),
        ],
        in_specs=[any_space] * 3,
        out_specs=[pl.BlockSpec(memory_space=pltpu.VMEM)] * 3,
        scratch_shapes=[
            pltpu.VMEM(halo, f32),
            pltpu.VMEM(pressure_now.shape, f32),
            pltpu.VMEM(pressure_now.shape, jnp.int32),
            pltpu.VMEM(halo, f32),
            pltpu.VMEM((3, rows, cols), f32),
            pltpu.VMEM((PIECES, 3, ROWS, cols), f32),
            pltpu.VMEM((PIECES, 3, ROWS, cols), f32),
            pltpu.VMEM((PIECES, chips, 3, ROWS, LANES), f32),
            pltpu.VMEM((3, rows, cols), f32),
            pltpu.SemaphoreType.DMA((PIECES,)),
            pltpu.SemaphoreType.DMA,
            pltpu.SemaphoreType.DMA((2,)),
            pltpu.SemaphoreType.DMA((2, 2, PIECES)),
            pltpu.SemaphoreType.DMA((2,)),
            pltpu.SemaphoreType.DMA((2, 2)),
            pltpu.SemaphoreType.DMA,
            pltpu.SemaphoreType.DMA((PIECES,)),
            pltpu.SemaphoreType.DMA,
            pltpu.SemaphoreType.DMA((PIECES,)),
            pltpu.SemaphoreType.DMA,
            pltpu.SemaphoreType.DMA((PIECES,)),
            pltpu.SemaphoreType.DMA,
            pltpu.SemaphoreType.DMA((PIECES,)),
        ],
        compiler_params=pltpu.CompilerParams(
            collective_id=0, has_side_effects=True, vmem_limit_bytes=48 * 1024 * 1024
        ),
    )(pressure_now, pressure_old, solid_flags)


def solution(mesh):
    return jax.shard_map(
        shards,
        mesh=mesh,
        in_specs=(P("depth", "tile", None), P("depth", "tile", None), P("depth", "tile", None)),
        out_specs=(P("depth", "tile", None), P("depth", "tile", None), P(None, "tile", None)),
        check_vma=False,
    )
```

```python
import functools
import math

import jax
import jax.numpy as jnp
from jax import lax
from jax.experimental import pallas as pl
from jax.experimental.pallas import tpu as pltpu
from jax.sharding import PartitionSpec as P

MESH = pl.DeviceIdType.MESH
LANES = 128
ROWS = 8
SPREAD = 8
PIECES = 4


def leap(before, field, closed, p, r, l):
    lane = lax.broadcasted_iota(jnp.int32, (ROWS, LANES), 1)
    row = lax.broadcasted_iota(jnp.int32, (ROWS, LANES), 0)

    def tile(dp=0, dr=0, dl=0):
        return field[p + dp, pl.ds(pl.multiple_of(r + dr, ROWS), ROWS), pl.ds(pl.multiple_of(l + dl, LANES), LANES)]

    here = tile()
    west = pltpu.roll(jnp.where(lane == LANES - 1, tile(dl=-LANES), here), 1, 1)
    east = pltpu.roll(jnp.where(lane == 0, tile(dl=LANES), here), LANES - 1, 1)
    north = pltpu.roll(jnp.where(row == ROWS - 1, tile(dr=-ROWS), here), 1, 0)
    south = pltpu.roll(jnp.where(row == 0, tile(dr=ROWS), here), ROWS - 1, 0)
    beside = (tile(dp=-1) + tile(dp=1)) + ((north + south) + (west + east))
    ahead = (0.2 * here - before) + 0.3 * beside
    return jnp.where(closed == 0, ahead, 0.0)


def kernel(
    steps, now_h, old_h, flag_h, mid, new, final,
    now, old, flag, part, peer, joint, shares,
    load_sem, face_send, face_recv, edge_send, edge_recv, pair_send, pair_recv,
    share_send, share_recv, spread_send, spread_recv, swap_send, swap_recv,
):
    depth_count, tile_count = lax.axis_size("depth"), lax.axis_size("tile")
    d, t = lax.axis_index("depth"), lax.axis_index("tile")
    planes, rows, cols = now_h.shape
    blocks, tiles = rows // ROWS, cols // LANES
    chips = depth_count // 2
    core, chip = lax.rem(d, 2), lax.div(d, 2)
    width = math.isqrt(chips)
    piece = rows // PIECES
    d_up, d_down = lax.rem(d + 1, depth_count), lax.rem(d + depth_count - 1, depth_count)
    t_up, t_down = lax.rem(t + 1, tile_count), lax.rem(t + tile_count - 1, tile_count)
    has_d_up, has_d_down = d < depth_count - 1, d > 0
    has_t_up, has_t_down = t < tile_count - 1, t > 0
    partner = d + 1 - 2 * core
    inner_rows, inner_cols = pl.ds(ROWS, rows), pl.ds(LANES, cols)
    near = (
        (has_d_up, (d_up, t)),
        (has_d_down, (d_down, t)),
        (has_t_up, (d, t_up)),
        (has_t_down, (d, t_down)),
    )

    barrier = pltpu.get_barrier_semaphore()
    for there, who in near:

        @pl.when(there)
        def _():
            pl.semaphore_signal(barrier, inc=1, device_id=who, device_id_type=MESH)

    def load(q):
        at = pl.ds(q * piece, piece)
        return [
            pltpu.make_async_copy(src.at[:, at], dst, load_sem.at[q])
            for src, dst in (
                (now_h, now.at[pl.ds(1, planes), pl.ds(ROWS + q * piece, piece), inner_cols]),
                (old_h, old.at[:, at]),
                (flag_h, flag.at[:, at]),
            )
        ]

    def await_load(q):
        three = old.at[:, pl.ds(0, 3 * piece)]
        pltpu.make_async_copy(three, three, load_sem.at[q]).wait()

    for q in range(PIECES):
        for copy in load(q):
            copy.start()

    for k in range(1, chips):
        other = lax.rem(chip + k, chips) * 2 + core
        pl.semaphore_signal(barrier, inc=1, device_id=(other, t), device_id_type=MESH)

    count = chips - 1
    for left in (d, depth_count - 1 - d, t, tile_count - 1 - t):
        count = count + jnp.minimum(left, 1)
    pl.semaphore_wait(barrier, count)

    def depth_face(stage, way, q):
        plane = (planes - 1) * way
        if stage == 0:
            src, field = now_h.at[plane, pl.ds(q * piece, piece)], now
        else:
            src, field = mid.at[plane + 1, pl.ds(ROWS + q * piece, piece), inner_cols], mid
        return pltpu.make_async_remote_copy(
            src_ref=src,
            dst_ref=field.at[(planes + 1) * (1 - way), pl.ds(ROWS + q * piece, piece), inner_cols],
            send_sem=face_send.at[way],
            recv_sem=face_recv.at[stage, way, q],
            device_id=((d_down, d_up)[way], t),
            device_id_type=MESH,
        )

    def tile_face(stage, way):
        row = (rows - 1) * way
        if stage == 0:
            src, field = now_h.at[:, pl.ds(row, 1)], now
        else:
            src, field = mid.at[pl.ds(1, planes), pl.ds(ROWS + row, 1), inner_cols], mid
        return pltpu.make_async_remote_copy(
            src_ref=src,
            dst_ref=field.at[pl.ds(1, planes), pl.ds(ROWS + rows if way == 0 else ROWS - 1, 1), inner_cols],
            send_sem=edge_send.at[way],
            recv_sem=edge_recv.at[stage, way],
            device_id=(d, (t_down, t_up)[way]),
            device_id_type=MESH,
        )

    d_to, t_to = (has_d_down, has_d_up), (has_t_down, has_t_up)
    d_from, t_from = d_to[::-1], t_to[::-1]

    def start_depth(stage, q):
        for way in range(2):
            pl.when(d_to[way])(lambda: depth_face(stage, way, q).start())

    def start_tile(stage, way):
        pl.when(t_to[way])(lambda: tile_face(stage, way).start())

    def await_depth(stage, q):
        for way in range(2):
            pl.when(d_from[way])(lambda: depth_face(stage, way, q).wait_recv())

    def await_tile(stage, way):
        pl.when(t_from[way])(lambda: tile_face(stage, way).wait_recv())

    for way in range(2):
        start_tile(0, way)
    for q in range(PIECES):
        start_depth(0, q)

    for field in (now, mid):
        for side in (0, LANES + cols):
            field[pl.ds(1, planes), inner_rows, pl.ds(side, LANES)] = jnp.zeros((planes, rows, LANES), jnp.float32)

        @pl.when(jnp.logical_not(has_d_down))
        def _():
            field[0, inner_rows, inner_cols] = jnp.zeros((rows, cols), jnp.float32)

        @pl.when(jnp.logical_not(has_d_up))
        def _():
            field[planes + 1, inner_rows, inner_cols] = jnp.zeros((rows, cols), jnp.float32)

        @pl.when(jnp.logical_not(has_t_down))
        def _():
            field[pl.ds(1, planes), pl.ds(0, ROWS), inner_cols] = jnp.zeros((planes, ROWS, cols), jnp.float32)

        @pl.when(jnp.logical_not(has_t_up))
        def _():
            field[pl.ds(1, planes), pl.ds(ROWS + rows, ROWS), inner_cols] = jnp.zeros((planes, ROWS, cols), jnp.float32)

    def over(count, body):
        turns = tiles // SPREAD

        def lap(n, carry):
            i, j = lax.div(n, turns), lax.rem(n, turns)
            for s in range(SPREAD):
                body(i, pl.multiple_of((j * SPREAD + s) * LANES, LANES))
            return carry

        lax.fori_loop(0, count * turns, lap, 0)

    def mid_tile(p, b, l):
        r = pl.multiple_of(b * ROWS, ROWS)
        here = (pl.ds(r, ROWS), pl.ds(l, LANES))
        mid[p + 1, pl.ds(pl.multiple_of(r + ROWS, ROWS), ROWS), pl.ds(pl.multiple_of(l + LANES, LANES), LANES)] = leap(
            old[(p,) + here], now, flag[(p,) + here], p + 1, r + ROWS, l + LANES
        )

    def mid_inner(b, l):
        for p in range(1, planes - 1):
            mid_tile(p, b, l)

    def mid_outer(b, l):
        for p in (0, planes - 1):
            mid_tile(p, b, l)

    rate = steps * math.log2(math.e)

    def new_tile(p, b, l):
        r = pl.multiple_of(b * ROWS, ROWS)
        here = (pl.ds(r, ROWS), pl.ds(l, LANES))
        before = now[p + 1, pl.ds(pl.multiple_of(r + ROWS, ROWS), ROWS), pl.ds(pl.multiple_of(l + LANES, LANES), LANES)]
        value = leap(before, mid, flag[(p,) + here], p + 1, r + ROWS, l + LANES)
        new[(p,) + here] = value
        square = value * value
        thick = square * pltpu.reciprocal(1.0 + square, approx=True)
        return thick, jnp.tanh(1.5 * value), jnp.exp2((-0.5 * math.log2(math.e)) * square)

    def place(b, l):
        return (pl.ds(pl.multiple_of(b * ROWS, ROWS), ROWS), pl.ds(l, LANES))

    def inner(b, l):
        at = place(b, l)
        depth = light = red = green = None
        for p in range(1, planes - 1):
            thick, warm, mild = new_tile(p, b, l)
            if depth is None:
                depth = thick
                after = jnp.exp2(-rate * depth)
                weight = 1.0 - after
                red, green = weight * warm, weight * mild
            else:
                depth = depth + thick
                after = jnp.exp2(-rate * depth)
                weight = light - after
                red, green = red + weight * warm, green + weight * mild
            light = after
        part[(0,) + at], part[(1,) + at], part[(2,) + at] = red, green, depth

    def outer(b, l):
        at = place(b, l)
        depth = part[(2,) + at]
        thick_a, warm_a, mild_a = new_tile(0, b, l)
        thick_b, warm_b, mild_b = new_tile(planes - 1, b, l)
        light_a = jnp.exp2(-rate * thick_a)
        depth_b = thick_a + depth
        light_b = jnp.exp2(-rate * depth_b)
        depth_c = depth_b + thick_b
        light_c = jnp.exp2(-rate * depth_c)
        weight_a, weight_b = 1.0 - light_a, light_b - light_c
        part[(0,) + at] = weight_a * warm_a + light_a * part[(0,) + at] + weight_b * warm_b
        part[(1,) + at] = weight_a * mild_a + light_a * part[(1,) + at] + weight_b * mild_b
        part[(2,) + at] = depth_c

    per = blocks // PIECES
    await_load(0)
    for q in range(1, PIECES):
        await_load(q)
        over(per, lambda i, l: mid_inner((q - 1) * per + 1 + i, l))
    for way in range(2):
        await_tile(0, way)
    over(2, lambda i, l: mid_inner(i * (blocks - 1), l))
    for q in range(PIECES):
        await_depth(0, q)
        over(per, lambda i, l: mid_outer(q * per + i, l))
        start_depth(1, q)
        if q == 0:
            start_tile(1, 0)
        else:
            if q == PIECES - 1:
                start_tile(1, 1)
            over(per, lambda i, l: inner((q - 1) * per + 1 + i, l))

    x, y = lax.div(chip, width), lax.rem(chip, width)
    own_tile = x * 2 + lax.div(y, 2)

    def owner(s, j):
        ox = lax.div(j, 2)
        return ox * width + 2 * lax.rem(j, 2) + lax.rem(ox + s, 2)

    def owns(s):
        return lax.rem(x + y + s, 2) == 0

    def block_rows(s, whose):
        return pl.ds(pl.multiple_of((2 * s + whose) * ROWS, ROWS), ROWS)

    def tile_cols(j):
        return pl.ds(pl.multiple_of(j * LANES, LANES), LANES)

    def pair(s):
        return pltpu.make_async_remote_copy(
            src_ref=part.at[:, block_rows(s, 1 - core)],
            dst_ref=peer.at[s],
            send_sem=pair_send,
            recv_sem=pair_recv.at[s],
            device_id=(partner, t),
            device_id_type=MESH,
        )

    def share(s, j):
        return pltpu.make_async_remote_copy(
            src_ref=joint.at[s, :, :, tile_cols(j)],
            dst_ref=shares.at[s, chip],
            send_sem=share_send,
            recv_sem=share_recv.at[s],
            device_id=(owner(s, j) * 2 + core, t),
            device_id_type=MESH,
        )

    def region(s, j):
        return final.at[:, block_rows(s, core), tile_cols(j)]

    def spread(s, who):
        return pltpu.make_async_remote_copy(
            src_ref=region(s, own_tile),
            dst_ref=region(s, own_tile),
            send_sem=spread_send,
            recv_sem=spread_recv.at[s],
            device_id=(who * 2 + core, t),
            device_id_type=MESH,
        )

    def swap(s, whose):
        at = final.at[:, block_rows(s, whose)]
        return pltpu.make_async_remote_copy(
            src_ref=at,
            dst_ref=at,
            send_sem=swap_send,
            recv_sem=swap_recv.at[s],
            device_id=(partner, t),
            device_id_type=MESH,
        )

    def await_tiles(sem, count):
        some = shares.at[pl.ds(0, 2), pl.ds(0, count // 2)] if count > chips else shares.at[0, pl.ds(0, count)]
        pltpu.make_async_copy(some, some, sem).wait()

    def shade(s):
        if s == 0:
            await_tile(1, 1)
            over(1, lambda _, l: inner(0, l))
        if s == PIECES - 1:
            await_tile(1, 0)
            over(1, lambda _, l: inner(blocks - 1, l))
        await_depth(1, s)
        over(1, lambda _, l: outer(2 * s + 1 - core, l))
        pair(s).start()
        over(1, lambda _, l: outer(2 * s + core, l))

    def join(s):
        pair(s).wait_recv()

        def merge(_, l):
            mine, first = (block_rows(s, core), pl.ds(l, LANES)), core == 0
            theirs = (slice(None), pl.ds(l, LANES))
            own = [part[(c,) + mine] for c in range(3)]
            other = [peer[(s, c) + theirs] for c in range(3)]
            light = jnp.exp2(-rate * jnp.where(first, own[2], other[2]))
            for c in range(2):
                joint[(s, c) + theirs] = jnp.where(first, own[c], other[c]) + light * jnp.where(first, other[c], own[c])
            joint[(s, 2) + theirs] = own[2] + other[2]

        over(1, merge)
        for k in range(tiles):
            j = lax.rem(chip + k, tiles)
            pl.when(owner(s, j) != chip)(lambda: share(s, j).start())

        @pl.when(owns(s))
        def _():
            for c in range(3):
                shares[s, chip, c] = joint[s, c, :, tile_cols(own_tile)]

    def compose(s):
        @pl.when(owns(s))
        def _():
            await_tiles(share_recv.at[s], chips - 1)
            red, green, depth = (shares[s, 0, c] for c in range(3))
            for k in range(1, chips):
                light = jnp.exp2(-rate * depth)
                red, green = red + light * shares[s, k, 0], green + light * shares[s, k, 1]
                depth = depth + shares[s, k, 2]
            opacity = 1.0 - jnp.exp2(-rate * depth)
            for c, value in enumerate((0.5 * (opacity + red), green, opacity)):
                final[c, block_rows(s, core), tile_cols(own_tile)] = value
            for k in range(1, chips):
                spread(s, lax.rem(chip + k, chips)).start()

    def gather(s):
        pl.when(owns(s))(lambda: await_tiles(spread_recv.at[s], tiles - 1))
        pl.when(jnp.logical_not(owns(s)))(lambda: await_tiles(spread_recv.at[s], tiles))
        swap(s, core).start()

    shade(0)
    for s in range(1, PIECES):
        shade(s)
        join(s - 1)
    join(PIECES - 1)
    for s in range(PIECES):
        compose(s)
    for s in range(PIECES):
        gather(s)
    for s in range(PIECES):
        swap(s, 1 - core).wait_recv()

    def sent(like, sem):
        pltpu.make_async_copy(like, like, sem).wait()

    for way in range(2):
        pl.when(d_to[way])(lambda: sent(now.at[pl.ds(0, 2), inner_rows, inner_cols], face_send.at[way]))
        pl.when(t_to[way])(lambda: sent(old.at[0, pl.ds(0, 2 * planes)], edge_send.at[way]))
    sent(peer, pair_send)
    await_tiles(share_send, PIECES * tiles - 2)
    await_tiles(spread_send, 2 * (chips - 1))
    sent(peer, swap_send)


def store(mid, new, final, mid_h, new_h, image_h, blue, sems):
    planes, rows, cols = new.shape
    pairs = (
        (final.at[0], image_h.at[0]),
        (final.at[1], image_h.at[1]),
        (final.at[2], image_h.at[3]),
        (mid.at[pl.ds(1, planes), pl.ds(ROWS, rows), pl.ds(LANES, cols)], mid_h),
        (new, new_h),
        (blue, image_h.at[2]),
    )
    copies = [pltpu.make_async_copy(src, dst, sems.at[i]) for i, (src, dst) in enumerate(pairs)]
    for copy in copies[:-1]:
        copy.start()
    blue[...] = final[2] - final[0]
    copies[-1].start()
    for copy in copies:
        copy.wait()


def shards(pressure_old, pressure_now, solid_flags):
    planes, rows, cols = pressure_now.shape
    chips = lax.axis_size("depth") // 2
    any_space = pl.BlockSpec(memory_space=pl.ANY)
    vmem_space = pl.BlockSpec(memory_space=pltpu.VMEM)
    f32 = jnp.float32
    halo = (planes + 2, rows + 2 * ROWS, cols + 2 * LANES)
    mid, new, final = pl.pallas_call(
        functools.partial(kernel, 4.0 / (planes * lax.axis_size("depth"))),
        out_shape=[
            jax.ShapeDtypeStruct(halo, f32),
            jax.ShapeDtypeStruct(pressure_now.shape, f32),
            jax.ShapeDtypeStruct((3, rows, cols), f32),
        ],
        in_specs=[any_space] * 3,
        out_specs=[vmem_space] * 3,
        scratch_shapes=[
            pltpu.VMEM(halo, f32),
            pltpu.VMEM(pressure_now.shape, f32),
            pltpu.VMEM(pressure_now.shape, jnp.int32),
            pltpu.VMEM((3, rows, cols), f32),
            pltpu.VMEM((PIECES, 3, ROWS, cols), f32),
            pltpu.VMEM((PIECES, 3, ROWS, cols), f32),
            pltpu.VMEM((PIECES, chips, 3, ROWS, LANES), f32),
            pltpu.SemaphoreType.DMA((PIECES,)),
            pltpu.SemaphoreType.DMA((2,)),
            pltpu.SemaphoreType.DMA((2, 2, PIECES)),
            pltpu.SemaphoreType.DMA((2,)),
            pltpu.SemaphoreType.DMA((2, 2)),
            pltpu.SemaphoreType.DMA,
            pltpu.SemaphoreType.DMA((PIECES,)),
            pltpu.SemaphoreType.DMA,
            pltpu.SemaphoreType.DMA((PIECES,)),
            pltpu.SemaphoreType.DMA,
            pltpu.SemaphoreType.DMA((PIECES,)),
            pltpu.SemaphoreType.DMA,
            pltpu.SemaphoreType.DMA((PIECES,)),
        ],
        compiler_params=pltpu.CompilerParams(
            collective_id=0, has_side_effects=True, vmem_limit_bytes=48 * 1024 * 1024
        ),
    )(pressure_now, pressure_old, solid_flags)
    return pl.pallas_call(
        store,
        out_shape=[
            jax.ShapeDtypeStruct(pressure_now.shape, f32),
            jax.ShapeDtypeStruct(pressure_now.shape, f32),
            jax.ShapeDtypeStruct((4, rows, cols), f32),
        ],
        in_specs=[vmem_space] * 3,
        out_specs=[any_space] * 3,
        scratch_shapes=[pltpu.VMEM((rows, cols), f32), pltpu.SemaphoreType.DMA((6,))],
    )(mid, new, final)


def solution(mesh):
    return jax.shard_map(
        shards,
        mesh=mesh,
        in_specs=(P("depth", "tile", None), P("depth", "tile", None), P("depth", "tile", None)),
        out_specs=(P("depth", "tile", None), P("depth", "tile", None), P(None, "tile", None)),
        check_vma=False,
    )
```

```python
import functools
import math

import jax
import jax.numpy as jnp
from jax import lax
from jax.experimental import pallas as pl
from jax.experimental.pallas import tpu as pltpu
from jax.sharding import PartitionSpec as P

MESH = pl.DeviceIdType.MESH
LANES = 128
ROWS = 8
SPREAD = 8
FAR_FIRST = (2, 1, 3, 0)
PIECES = 4


def leap(before, field, closed, p, r, l, above=True, below=True):
    lane = lax.broadcasted_iota(jnp.int32, (ROWS, LANES), 1)
    row = lax.broadcasted_iota(jnp.int32, (ROWS, LANES), 0)

    def tile(dp=0, dr=0, dl=0):
        return field[p + dp, pl.ds(pl.multiple_of(r + dr, ROWS), ROWS), pl.ds(pl.multiple_of(l + dl, LANES), LANES)]

    here = tile()
    west = pltpu.roll(jnp.where(lane == LANES - 1, tile(dl=-LANES), here), 1, 1)
    east = pltpu.roll(jnp.where(lane == 0, tile(dl=LANES), here), LANES - 1, 1)
    north = pltpu.roll(jnp.where(row == ROWS - 1, tile(dr=-ROWS), here) if above else here, 1, 0)
    south = pltpu.roll(jnp.where(row == 0, tile(dr=ROWS), here) if below else here, ROWS - 1, 0)
    beside = (tile(dp=-1) + tile(dp=1)) + ((north + south) + (west + east))
    ahead = (0.2 * here - before) + 0.3 * beside
    return jnp.where(closed == 0, ahead, 0.0)


def kernel(
    steps, now_h, old_h, flag_h, mid_out, new, image,
    now, old, flag, mid, part, peer, joint, shares, final,
    load_sem, store_sem, face_send, face_recv, edge_send, edge_recv, pair_send, pair_recv,
    share_send, share_recv, spread_send, spread_recv, swap_send, swap_recv,
):
    depth_count, tile_count = lax.axis_size("depth"), lax.axis_size("tile")
    d, t = lax.axis_index("depth"), lax.axis_index("tile")
    planes, rows, cols = now_h.shape
    blocks, tiles = rows // ROWS, cols // LANES
    chips = depth_count // 2
    core, chip = lax.rem(d, 2), lax.div(d, 2)
    width = math.isqrt(chips)
    piece = rows // PIECES
    d_up, d_down = lax.rem(d + 1, depth_count), lax.rem(d + depth_count - 1, depth_count)
    t_up, t_down = lax.rem(t + 1, tile_count), lax.rem(t + tile_count - 1, tile_count)
    has_d_up, has_d_down = d < depth_count - 1, d > 0
    has_t_up, has_t_down = t < tile_count - 1, t > 0
    partner = d + 1 - 2 * core
    inner_rows, inner_cols = pl.ds(ROWS, rows), pl.ds(LANES, cols)
    near = (
        (has_d_up, (d_up, t)),
        (has_d_down, (d_down, t)),
        (has_t_up, (d, t_up)),
        (has_t_down, (d, t_down)),
    )

    barrier = pltpu.get_barrier_semaphore()
    for there, who in near:

        @pl.when(there)
        def _():
            pl.semaphore_signal(barrier, inc=1, device_id=who, device_id_type=MESH)

    def load(q):
        at = pl.ds(q * piece, piece)
        return [
            pltpu.make_async_copy(src.at[:, at], dst, load_sem.at[q])
            for src, dst in (
                (now_h, now.at[pl.ds(1, planes), pl.ds(ROWS + q * piece, piece), inner_cols]),
                (old_h, old.at[:, at]),
                (flag_h, flag.at[:, at]),
            )
        ]

    def await_load(q):
        three = old.at[:, pl.ds(0, 3 * piece)]
        pltpu.make_async_copy(three, three, load_sem.at[q]).wait()

    for q in range(PIECES):
        for copy in load(q):
            copy.start()

    for k in range(1, chips):
        other = lax.rem(chip + k, chips) * 2 + core
        pl.semaphore_signal(barrier, inc=1, device_id=(other, t), device_id_type=MESH)

    count = chips - 1
    for left in (d, depth_count - 1 - d, t, tile_count - 1 - t):
        count = count + jnp.minimum(left, 1)
    pl.semaphore_wait(barrier, count)

    def depth_face(stage, way, q):
        plane = (planes - 1) * way
        if stage == 0:
            src, field = now_h.at[plane, pl.ds(q * piece, piece)], now
        else:
            src, field = mid.at[plane + 1, pl.ds(ROWS + q * piece, piece), inner_cols], mid
        return pltpu.make_async_remote_copy(
            src_ref=src,
            dst_ref=field.at[(planes + 1) * (1 - way), pl.ds(ROWS + q * piece, piece), inner_cols],
            send_sem=face_send.at[way],
            recv_sem=face_recv.at[stage, way, q],
            device_id=((d_down, d_up)[way], t),
            device_id_type=MESH,
        )

    def tile_face(stage, way):
        row = (rows - 1) * way
        if stage == 0:
            src, field = now_h.at[:, pl.ds(row, 1)], now
        else:
            src, field = mid.at[pl.ds(1, planes), pl.ds(ROWS + row, 1), inner_cols], mid
        return pltpu.make_async_remote_copy(
            src_ref=src,
            dst_ref=field.at[pl.ds(1, planes), pl.ds(ROWS + rows if way == 0 else ROWS - 1, 1), inner_cols],
            send_sem=edge_send.at[way],
            recv_sem=edge_recv.at[stage, way],
            device_id=(d, (t_down, t_up)[way]),
            device_id_type=MESH,
        )

    d_to, t_to = (has_d_down, has_d_up), (has_t_down, has_t_up)
    d_from, t_from = d_to[::-1], t_to[::-1]

    def start_depth(stage, q):
        for way in range(2):
            pl.when(d_to[way])(lambda: depth_face(stage, way, q).start())

    def start_tile(stage, way):
        pl.when(t_to[way])(lambda: tile_face(stage, way).start())

    def await_depth(stage, q):
        for way in range(2):
            pl.when(d_from[way])(lambda: depth_face(stage, way, q).wait_recv())

    def await_tile(stage, way):
        pl.when(t_from[way])(lambda: tile_face(stage, way).wait_recv())

    for way in range(2):
        start_tile(0, way)
    for q in range(PIECES):
        start_depth(0, q)

    for field in (now, mid):
        for side in (0, LANES + cols):
            field[pl.ds(1, planes), inner_rows, pl.ds(side, LANES)] = jnp.zeros((planes, rows, LANES), jnp.float32)

        @pl.when(jnp.logical_not(has_d_down))
        def _():
            field[0, inner_rows, inner_cols] = jnp.zeros((rows, cols), jnp.float32)

        @pl.when(jnp.logical_not(has_d_up))
        def _():
            field[planes + 1, inner_rows, inner_cols] = jnp.zeros((rows, cols), jnp.float32)

        @pl.when(jnp.logical_not(has_t_down))
        def _():
            field[pl.ds(1, planes), pl.ds(0, ROWS), inner_cols] = jnp.zeros((planes, ROWS, cols), jnp.float32)

        @pl.when(jnp.logical_not(has_t_up))
        def _():
            field[pl.ds(1, planes), pl.ds(ROWS + rows, ROWS), inner_cols] = jnp.zeros((planes, ROWS, cols), jnp.float32)

    def over(count, body):
        turns = tiles // SPREAD

        def lap(n, carry):
            i, j = lax.div(n, turns), lax.rem(n, turns)
            for s in range(SPREAD):
                body(i, pl.multiple_of((j * SPREAD + s) * LANES, LANES))
            return carry

        lax.fori_loop(0, count * turns, lap, 0)

    def mid_tile(p, b, l, above=True, below=True):
        r = pl.multiple_of(b * ROWS, ROWS)
        here = (pl.ds(r, ROWS), pl.ds(l, LANES))
        mid[p + 1, pl.ds(pl.multiple_of(r + ROWS, ROWS), ROWS), pl.ds(pl.multiple_of(l + LANES, LANES), LANES)] = leap(
            old[(p,) + here], now, flag[(p,) + here], p + 1, r + ROWS, l + LANES, above, below
        )

    def mid_blocks(first, count, chosen, above=True, below=True):
        def body(i, l):
            for p in chosen:
                mid_tile(p, first + i, l, above, below)

        over(count, body)

    rate = steps * math.log2(math.e)

    def new_tile(p, b, l):
        r = pl.multiple_of(b * ROWS, ROWS)
        here = (pl.ds(r, ROWS), pl.ds(l, LANES))
        before = now[p + 1, pl.ds(pl.multiple_of(r + ROWS, ROWS), ROWS), pl.ds(pl.multiple_of(l + LANES, LANES), LANES)]
        value = leap(before, mid, flag[(p,) + here], p + 1, r + ROWS, l + LANES)
        new[(p,) + here] = value
        square = value * value
        thick = square * pltpu.reciprocal(1.0 + square, approx=True)
        return thick, jnp.tanh(1.5 * value), jnp.exp2((-0.5 * math.log2(math.e)) * square)

    def place(b, l):
        return (pl.ds(pl.multiple_of(b * ROWS, ROWS), ROWS), pl.ds(l, LANES))

    def inner(b, l):
        at = place(b, l)
        depth = light = red = green = None
        for p in range(1, planes - 1):
            thick, warm, mild = new_tile(p, b, l)
            if depth is None:
                depth = thick
                after = jnp.exp2(-rate * depth)
                weight = 1.0 - after
                red, green = weight * warm, weight * mild
            else:
                depth = depth + thick
                after = jnp.exp2(-rate * depth)
                weight = light - after
                red, green = red + weight * warm, green + weight * mild
            light = after
        part[(0,) + at], part[(1,) + at], part[(2,) + at] = red, green, depth

    def outer(b, l):
        at = place(b, l)
        depth = part[(2,) + at]
        thick_a, warm_a, mild_a = new_tile(0, b, l)
        thick_b, warm_b, mild_b = new_tile(planes - 1, b, l)
        light_a = jnp.exp2(-rate * thick_a)
        depth_b = thick_a + depth
        light_b = jnp.exp2(-rate * depth_b)
        depth_c = depth_b + thick_b
        light_c = jnp.exp2(-rate * depth_c)
        weight_a, weight_b = 1.0 - light_a, light_b - light_c
        part[(0,) + at] = weight_a * warm_a + light_a * part[(0,) + at] + weight_b * warm_b
        part[(1,) + at] = weight_a * mild_a + light_a * part[(1,) + at] + weight_b * mild_b
        part[(2,) + at] = depth_c

    within, ends = range(1, planes - 1), (0, planes - 1)
    last = blocks - 1
    await_load(0)
    mid_blocks(0, 1, within, above=False)
    for q in range(1, PIECES):
        await_load(q)
        mid_blocks(2 * q - 1, 2, within)
    mid_blocks(last, 1, within, below=False)
    for q in range(PIECES):
        await_depth(0, q)
        if q == 0:
            mid_blocks(0, 1, ends, above=False)
            mid_blocks(1, 1, ends)
            continue
        if q < PIECES - 1:
            mid_blocks(2 * q, 2, ends)
            start_depth(1, q)
        else:
            mid_blocks(2 * q, 1, ends)
            await_tile(0, 0)
            mid_blocks(last, 1, range(planes))
            start_depth(1, q)
            start_tile(1, 1)
        over(2, lambda i, l: inner(2 * q - 1 + i, l))
        if q == PIECES - 2:
            await_tile(0, 1)
            mid_blocks(0, 1, range(planes))
            start_depth(1, 0)
            start_tile(1, 0)
    mid_store = pltpu.make_async_copy(mid.at[pl.ds(1, planes), inner_rows, inner_cols], mid_out, store_sem)
    mid_store.start()

    x, y = lax.div(chip, width), lax.rem(chip, width)
    own_tile = x * 2 + lax.div(y, 2)

    def owner(s, j):
        ox = lax.div(j, 2)
        return ox * width + 2 * lax.rem(j, 2) + lax.rem(ox + s, 2)

    def owns(s):
        return lax.rem(x + y + s, 2) == 0

    def block_rows(s, whose):
        return pl.ds(pl.multiple_of((2 * s + whose) * ROWS, ROWS), ROWS)

    def tile_cols(j):
        return pl.ds(pl.multiple_of(j * LANES, LANES), LANES)

    def pair(s):
        return pltpu.make_async_remote_copy(
            src_ref=part.at[:, block_rows(s, 1 - core)],
            dst_ref=peer.at[s],
            send_sem=pair_send,
            recv_sem=pair_recv.at[s],
            device_id=(partner, t),
            device_id_type=MESH,
        )

    def share(s, j):
        return pltpu.make_async_remote_copy(
            src_ref=joint.at[s, :, :, tile_cols(j)],
            dst_ref=shares.at[s, chip],
            send_sem=share_send,
            recv_sem=share_recv.at[s],
            device_id=(owner(s, j) * 2 + core, t),
            device_id_type=MESH,
        )

    def region(s, j):
        return final.at[:, block_rows(s, core), tile_cols(j)]

    def spread(s, who):
        return pltpu.make_async_remote_copy(
            src_ref=region(s, own_tile),
            dst_ref=region(s, own_tile),
            send_sem=spread_send,
            recv_sem=spread_recv.at[s],
            device_id=(who * 2 + core, t),
            device_id_type=MESH,
        )

    def swap(s, whose):
        at = final.at[:, block_rows(s, whose)]
        return pltpu.make_async_remote_copy(
            src_ref=at,
            dst_ref=at,
            send_sem=swap_send,
            recv_sem=swap_recv.at[s],
            device_id=(partner, t),
            device_id_type=MESH,
        )

    def await_tiles(sem, count):
        some = shares.at[pl.ds(0, 2), pl.ds(0, count // 2)] if count > chips else shares.at[0, pl.ds(0, count)]
        pltpu.make_async_copy(some, some, sem).wait()

    def shade(s):
        if s == 0:
            await_tile(1, 1)
            over(1, lambda _, l: inner(0, l))
        if s == PIECES - 1:
            await_tile(1, 0)
            over(1, lambda _, l: inner(blocks - 1, l))
        await_depth(1, s)
        over(1, lambda _, l: outer(2 * s + 1 - core, l))
        pair(s).start()
        over(1, lambda _, l: outer(2 * s + core, l))

    def join(s):
        pair(s).wait_recv()

        def merge(_, l):
            mine, first = (block_rows(s, core), pl.ds(l, LANES)), core == 0
            theirs = (slice(None), pl.ds(l, LANES))
            own = [part[(c,) + mine] for c in range(3)]
            other = [peer[(s, c) + theirs] for c in range(3)]
            light = jnp.exp2(-rate * jnp.where(first, own[2], other[2]))
            for c in range(2):
                joint[(s, c) + theirs] = jnp.where(first, own[c], other[c]) + light * jnp.where(first, other[c], own[c])
            joint[(s, 2) + theirs] = own[2] + other[2]

        over(1, merge)
        for dx in FAR_FIRST:
            for m in range(2):
                j = 2 * lax.rem(x + dx, width) + lax.rem(lax.div(y, 2) + 1 + m, 2)
                pl.when(owner(s, j) != chip)(lambda: share(s, j).start())

        @pl.when(owns(s))
        def _():
            for c in range(3):
                shares[s, chip, c] = joint[s, c, :, tile_cols(own_tile)]

    def compose(s):
        @pl.when(owns(s))
        def _():
            await_tiles(share_recv.at[s], chips - 1)
            red, green, depth = (shares[s, 0, c] for c in range(3))
            for k in range(1, chips):
                light = jnp.exp2(-rate * depth)
                red, green = red + light * shares[s, k, 0], green + light * shares[s, k, 1]
                depth = depth + shares[s, k, 2]
            opacity = 1.0 - jnp.exp2(-rate * depth)
            for c, value in enumerate((0.5 * (opacity + red), green, opacity)):
                final[c, block_rows(s, core), tile_cols(own_tile)] = value
            for dx in FAR_FIRST:
                for dy in FAR_FIRST:
                    if dx or dy:
                        spread(s, lax.rem(x + dx, width) * width + lax.rem(y + dy, width)).start()

    def gather(s):
        pl.when(owns(s))(lambda: await_tiles(spread_recv.at[s], tiles - 1))
        pl.when(jnp.logical_not(owns(s)))(lambda: await_tiles(spread_recv.at[s], tiles))
        swap(s, core).start()

    def finish(s):
        swap(s, 1 - core).wait_recv()
        at = pl.ds(2 * s * ROWS, 2 * ROWS)
        red, green, opacity = (final[c, at] for c in range(3))
        for c, value in enumerate((red, green, opacity - red, opacity)):
            image[c, at] = value

    order = (1, 2, 0, 3)
    shade(order[0])
    for earlier, s in zip(order, order[1:]):
        shade(s)
        join(earlier)
    join(order[-1])
    for s in order:
        compose(s)
    gather(order[0])
    for earlier, s in zip(order, order[1:]):
        gather(s)
        finish(earlier)
    finish(order[-1])

    def sent(like, sem):
        pltpu.make_async_copy(like, like, sem).wait()

    for way in range(2):
        pl.when(d_to[way])(lambda: sent(now.at[pl.ds(0, 2), inner_rows, inner_cols], face_send.at[way]))
        pl.when(t_to[way])(lambda: sent(old.at[0, pl.ds(0, 2 * planes)], edge_send.at[way]))
    sent(peer, pair_send)
    await_tiles(share_send, PIECES * tiles - 2)
    await_tiles(spread_send, 2 * (chips - 1))
    sent(peer, swap_send)
    mid_store.wait()


def shards(pressure_old, pressure_now, solid_flags):
    planes, rows, cols = pressure_now.shape
    chips = lax.axis_size("depth") // 2
    any_space = pl.BlockSpec(memory_space=pl.ANY)
    f32 = jnp.float32
    halo = (planes + 2, rows + 2 * ROWS, cols + 2 * LANES)
    return pl.pallas_call(
        functools.partial(kernel, 4.0 / (planes * lax.axis_size("depth"))),
        out_shape=[
            jax.ShapeDtypeStruct(pressure_now.shape, f32),
            jax.ShapeDtypeStruct(pressure_now.shape, f32),
            jax.ShapeDtypeStruct((4, rows, cols), f32),
        ],
        in_specs=[any_space] * 3,
        out_specs=[pl.BlockSpec(memory_space=pltpu.VMEM)] * 3,
        scratch_shapes=[
            pltpu.VMEM(halo, f32),
            pltpu.VMEM(pressure_now.shape, f32),
            pltpu.VMEM(pressure_now.shape, jnp.int32),
            pltpu.VMEM(halo, f32),
            pltpu.VMEM((3, rows, cols), f32),
            pltpu.VMEM((PIECES, 3, ROWS, cols), f32),
            pltpu.VMEM((PIECES, 3, ROWS, cols), f32),
            pltpu.VMEM((PIECES, chips, 3, ROWS, LANES), f32),
            pltpu.VMEM((3, rows, cols), f32),
            pltpu.SemaphoreType.DMA((PIECES,)),
            pltpu.SemaphoreType.DMA,
            pltpu.SemaphoreType.DMA((2,)),
            pltpu.SemaphoreType.DMA((2, 2, PIECES)),
            pltpu.SemaphoreType.DMA((2,)),
            pltpu.SemaphoreType.DMA((2, 2)),
            pltpu.SemaphoreType.DMA,
            pltpu.SemaphoreType.DMA((PIECES,)),
            pltpu.SemaphoreType.DMA,
            pltpu.SemaphoreType.DMA((PIECES,)),
            pltpu.SemaphoreType.DMA,
            pltpu.SemaphoreType.DMA((PIECES,)),
            pltpu.SemaphoreType.DMA,
            pltpu.SemaphoreType.DMA((PIECES,)),
        ],
        compiler_params=pltpu.CompilerParams(
            collective_id=0, has_side_effects=True, vmem_limit_bytes=48 * 1024 * 1024
        ),
    )(pressure_now, pressure_old, solid_flags)


def solution(mesh):
    return jax.shard_map(
        shards,
        mesh=mesh,
        in_specs=(P("depth", "tile", None), P("depth", "tile", None), P("depth", "tile", None)),
        out_specs=(P("depth", "tile", None), P("depth", "tile", None), P(None, "tile", None)),
        check_vma=False,
    )
```

```python
import functools
import math

import jax
import jax.numpy as jnp
from jax import lax
from jax.experimental import pallas as pl
from jax.experimental.pallas import tpu as pltpu
from jax.sharding import PartitionSpec as P

MESH = pl.DeviceIdType.MESH
LANES = 128
ROWS = 8
SPREAD = 8
FAR_FIRST = (2, 1, 3, 0)
PIECES = 4


def leap(before, field, closed, p, r, l, above=True, below=True):
    lane = lax.broadcasted_iota(jnp.int32, (ROWS, LANES), 1)
    row = lax.broadcasted_iota(jnp.int32, (ROWS, LANES), 0)

    def tile(dp=0, dr=0, dl=0):
        return field[p + dp, pl.ds(pl.multiple_of(r + dr, ROWS), ROWS), pl.ds(pl.multiple_of(l + dl, LANES), LANES)]

    here = tile()
    west = pltpu.roll(jnp.where(lane == LANES - 1, tile(dl=-LANES), here), 1, 1)
    east = pltpu.roll(jnp.where(lane == 0, tile(dl=LANES), here), LANES - 1, 1)
    north = pltpu.roll(jnp.where(row == ROWS - 1, tile(dr=-ROWS), here) if above else here, 1, 0)
    south = pltpu.roll(jnp.where(row == 0, tile(dr=ROWS), here) if below else here, ROWS - 1, 0)
    beside = (tile(dp=-1) + tile(dp=1)) + ((north + south) + (west + east))
    ahead = (0.2 * here - before) + 0.3 * beside
    return jnp.where(closed == 0, ahead, 0.0)


def kernel(
    steps, now_h, old_h, flag_h, mid_out, new, image,
    now, old, flag, mid, part, peer, joint, shares, final,
    load_sem, store_sem, face_send, face_recv, edge_send, edge_recv, pair_send, pair_recv,
    share_send, share_recv, spread_send, spread_recv, swap_send, swap_recv,
):
    depth_count, tile_count = lax.axis_size("depth"), lax.axis_size("tile")
    d, t = lax.axis_index("depth"), lax.axis_index("tile")
    planes, rows, cols = now_h.shape
    blocks, tiles = rows // ROWS, cols // LANES
    chips = depth_count // 2
    core, chip = lax.rem(d, 2), lax.div(d, 2)
    width = math.isqrt(chips)
    piece = rows // PIECES
    d_up, d_down = lax.rem(d + 1, depth_count), lax.rem(d + depth_count - 1, depth_count)
    t_up, t_down = lax.rem(t + 1, tile_count), lax.rem(t + tile_count - 1, tile_count)
    has_d_up, has_d_down = d < depth_count - 1, d > 0
    has_t_up, has_t_down = t < tile_count - 1, t > 0
    partner = d + 1 - 2 * core
    inner_rows, inner_cols = pl.ds(ROWS, rows), pl.ds(LANES, cols)
    near = (
        (has_d_up, (d_up, t)),
        (has_d_down, (d_down, t)),
        (has_t_up, (d, t_up)),
        (has_t_down, (d, t_down)),
    )

    barrier = pltpu.get_barrier_semaphore()
    x, y = lax.div(chip, width), lax.rem(chip, width)
    for dx in FAR_FIRST:
        for dy in FAR_FIRST:
            if dx or dy:
                other = lax.rem(x + dx, width) * width + lax.rem(y + dy, width)
                pl.semaphore_signal(barrier, inc=1, device_id=(other * 2 + core, t), device_id_type=MESH)
    for there, who in near:

        @pl.when(there)
        def _():
            pl.semaphore_signal(barrier, inc=1, device_id=who, device_id_type=MESH)

    def load(q):
        at = pl.ds(q * piece, piece)
        return [
            pltpu.make_async_copy(src.at[:, at], dst, load_sem.at[q])
            for src, dst in (
                (now_h, now.at[pl.ds(1, planes), pl.ds(ROWS + q * piece, piece), inner_cols]),
                (old_h, old.at[:, at]),
                (flag_h, flag.at[:, at]),
            )
        ]

    def await_load(q):
        three = old.at[:, pl.ds(0, 3 * piece)]
        pltpu.make_async_copy(three, three, load_sem.at[q]).wait()

    for q in range(PIECES):
        for copy in load(q):
            copy.start()

    count = chips - 1
    for left in (d, depth_count - 1 - d, t, tile_count - 1 - t):
        count = count + jnp.minimum(left, 1)
    pl.semaphore_wait(barrier, count)

    def depth_face(stage, way, q):
        plane = (planes - 1) * way
        if stage == 0:
            src, field = now_h.at[plane, pl.ds(q * piece, piece)], now
        else:
            src, field = mid.at[plane + 1, pl.ds(ROWS + q * piece, piece), inner_cols], mid
        return pltpu.make_async_remote_copy(
            src_ref=src,
            dst_ref=field.at[(planes + 1) * (1 - way), pl.ds(ROWS + q * piece, piece), inner_cols],
            send_sem=face_send.at[way],
            recv_sem=face_recv.at[stage, way, q],
            device_id=((d_down, d_up)[way], t),
            device_id_type=MESH,
        )

    def tile_face(stage, way):
        row = (rows - 1) * way
        if stage == 0:
            src, field = now_h.at[:, pl.ds(row, 1)], now
        else:
            src, field = mid.at[pl.ds(1, planes), pl.ds(ROWS + row, 1), inner_cols], mid
        return pltpu.make_async_remote_copy(
            src_ref=src,
            dst_ref=field.at[pl.ds(1, planes), pl.ds(ROWS + rows if way == 0 else ROWS - 1, 1), inner_cols],
            send_sem=edge_send.at[way],
            recv_sem=edge_recv.at[stage, way],
            device_id=(d, (t_down, t_up)[way]),
            device_id_type=MESH,
        )

    d_to, t_to = (has_d_down, has_d_up), (has_t_down, has_t_up)
    d_from, t_from = d_to[::-1], t_to[::-1]

    def start_depth(stage, q):
        for way in range(2):
            pl.when(d_to[way])(lambda: depth_face(stage, way, q).start())

    def start_tile(stage, way):
        pl.when(t_to[way])(lambda: tile_face(stage, way).start())

    def await_depth(stage, q):
        for way in range(2):
            pl.when(d_from[way])(lambda: depth_face(stage, way, q).wait_recv())

    def await_tile(stage, way):
        pl.when(t_from[way])(lambda: tile_face(stage, way).wait_recv())

    for way in range(2):
        start_tile(0, way)
    for q in range(PIECES):
        start_depth(0, q)

    for field in (now, mid):
        for side in (0, LANES + cols):
            field[pl.ds(1, planes), inner_rows, pl.ds(side, LANES)] = jnp.zeros((planes, rows, LANES), jnp.float32)

        @pl.when(jnp.logical_not(has_d_down))
        def _():
            field[0, inner_rows, inner_cols] = jnp.zeros((rows, cols), jnp.float32)

        @pl.when(jnp.logical_not(has_d_up))
        def _():
            field[planes + 1, inner_rows, inner_cols] = jnp.zeros((rows, cols), jnp.float32)

        @pl.when(jnp.logical_not(has_t_down))
        def _():
            field[pl.ds(1, planes), pl.ds(0, ROWS), inner_cols] = jnp.zeros((planes, ROWS, cols), jnp.float32)

        @pl.when(jnp.logical_not(has_t_up))
        def _():
            field[pl.ds(1, planes), pl.ds(ROWS + rows, ROWS), inner_cols] = jnp.zeros((planes, ROWS, cols), jnp.float32)

    def over(count, body):
        turns = tiles // SPREAD

        def lap(n, carry):
            i, j = lax.div(n, turns), lax.rem(n, turns)
            for s in range(SPREAD):
                body(i, pl.multiple_of((j * SPREAD + s) * LANES, LANES))
            return carry

        lax.fori_loop(0, count * turns, lap, 0)

    def mid_tile(p, b, l, above=True, below=True):
        r = pl.multiple_of(b * ROWS, ROWS)
        here = (pl.ds(r, ROWS), pl.ds(l, LANES))
        mid[p + 1, pl.ds(pl.multiple_of(r + ROWS, ROWS), ROWS), pl.ds(pl.multiple_of(l + LANES, LANES), LANES)] = leap(
            old[(p,) + here], now, flag[(p,) + here], p + 1, r + ROWS, l + LANES, above, below
        )

    def mid_blocks(first, count, chosen, above=True, below=True):
        def body(i, l):
            for p in chosen:
                mid_tile(p, first + i, l, above, below)

        over(count, body)

    rate = steps * math.log2(math.e)

    def new_tile(p, b, l):
        r = pl.multiple_of(b * ROWS, ROWS)
        here = (pl.ds(r, ROWS), pl.ds(l, LANES))
        before = now[p + 1, pl.ds(pl.multiple_of(r + ROWS, ROWS), ROWS), pl.ds(pl.multiple_of(l + LANES, LANES), LANES)]
        value = leap(before, mid, flag[(p,) + here], p + 1, r + ROWS, l + LANES)
        new[(p,) + here] = value
        square = value * value
        thick = square * pltpu.reciprocal(1.0 + square, approx=True)
        return thick, jnp.tanh(1.5 * value), jnp.exp2((-0.5 * math.log2(math.e)) * square)

    def place(b, l):
        return (pl.ds(pl.multiple_of(b * ROWS, ROWS), ROWS), pl.ds(l, LANES))

    def inner(b, l):
        at = place(b, l)
        depth = light = red = green = None
        for p in range(1, planes - 1):
            thick, warm, mild = new_tile(p, b, l)
            if depth is None:
                depth = thick
                after = jnp.exp2(-rate * depth)
                weight = 1.0 - after
                red, green = weight * warm, weight * mild
            else:
                depth = depth + thick
                after = jnp.exp2(-rate * depth)
                weight = light - after
                red, green = red + weight * warm, green + weight * mild
            light = after
        part[(0,) + at], part[(1,) + at], part[(2,) + at] = red, green, depth

    def outer(b, l):
        at = place(b, l)
        depth = part[(2,) + at]
        thick_a, warm_a, mild_a = new_tile(0, b, l)
        thick_b, warm_b, mild_b = new_tile(planes - 1, b, l)
        light_a = jnp.exp2(-rate * thick_a)
        depth_b = thick_a + depth
        light_b = jnp.exp2(-rate * depth_b)
        depth_c = depth_b + thick_b
        light_c = jnp.exp2(-rate * depth_c)
        weight_a, weight_b = 1.0 - light_a, light_b - light_c
        part[(0,) + at] = weight_a * warm_a + light_a * part[(0,) + at] + weight_b * warm_b
        part[(1,) + at] = weight_a * mild_a + light_a * part[(1,) + at] + weight_b * mild_b
        part[(2,) + at] = depth_c

    within, ends = range(1, planes - 1), (0, planes - 1)
    last = blocks - 1
    await_load(0)
    mid_blocks(0, 1, within, above=False)
    for q in range(1, PIECES):
        await_load(q)
        mid_blocks(2 * q - 1, 2, within)
    mid_blocks(last, 1, within, below=False)
    for q in range(PIECES):
        await_depth(0, q)
        if q == 0:
            mid_blocks(0, 1, ends, above=False)
            mid_blocks(1, 1, ends)
            continue
        if q < PIECES - 1:
            mid_blocks(2 * q, 2, ends)
            start_depth(1, q)
        else:
            mid_blocks(2 * q, 1, ends)
            await_tile(0, 0)
            mid_blocks(last, 1, range(planes))
            start_depth(1, q)
            start_tile(1, 1)
        over(2, lambda i, l: inner(2 * q - 1 + i, l))
        if q == PIECES - 2:
            await_tile(0, 1)
            mid_blocks(0, 1, range(planes))
            start_depth(1, 0)
            start_tile(1, 0)
    mid_store = pltpu.make_async_copy(mid.at[pl.ds(1, planes), inner_rows, inner_cols], mid_out, store_sem)
    mid_store.start()

    own_tile = x * 2 + lax.div(y, 2)

    def owner(s, j):
        ox = lax.div(j, 2)
        return ox * width + 2 * lax.rem(j, 2) + lax.rem(ox + s, 2)

    def owns(s):
        return lax.rem(x + y + s, 2) == 0

    def block_rows(s, whose):
        return pl.ds(pl.multiple_of((2 * s + whose) * ROWS, ROWS), ROWS)

    def tile_cols(j):
        return pl.ds(pl.multiple_of(j * LANES, LANES), LANES)

    def pair(s):
        return pltpu.make_async_remote_copy(
            src_ref=part.at[:, block_rows(s, 1 - core)],
            dst_ref=peer.at[s],
            send_sem=pair_send,
            recv_sem=pair_recv.at[s],
            device_id=(partner, t),
            device_id_type=MESH,
        )

    def share(s, j):
        return pltpu.make_async_remote_copy(
            src_ref=joint.at[s, :, :, tile_cols(j)],
            dst_ref=shares.at[s, chip],
            send_sem=share_send,
            recv_sem=share_recv.at[s],
            device_id=(owner(s, j) * 2 + core, t),
            device_id_type=MESH,
        )

    def region(s, j):
        return final.at[:, block_rows(s, core), tile_cols(j)]

    def spread(s, who):
        return pltpu.make_async_remote_copy(
            src_ref=region(s, own_tile),
            dst_ref=region(s, own_tile),
            send_sem=spread_send,
            recv_sem=spread_recv.at[s],
            device_id=(who * 2 + core, t),
            device_id_type=MESH,
        )

    def swap(s, whose):
        at = final.at[:, block_rows(s, whose)]
        return pltpu.make_async_remote_copy(
            src_ref=at,
            dst_ref=at,
            send_sem=swap_send,
            recv_sem=swap_recv.at[s],
            device_id=(partner, t),
            device_id_type=MESH,
        )

    def await_tiles(sem, count):
        some = shares.at[pl.ds(0, 2), pl.ds(0, count // 2)] if count > chips else shares.at[0, pl.ds(0, count)]
        pltpu.make_async_copy(some, some, sem).wait()

    def shade(s):
        if s == 0:
            await_tile(1, 1)
            over(1, lambda _, l: inner(0, l))
        if s == PIECES - 1:
            await_tile(1, 0)
            over(1, lambda _, l: inner(blocks - 1, l))
        await_depth(1, s)
        over(1, lambda _, l: outer(2 * s + 1 - core, l))
        pair(s).start()
        over(1, lambda _, l: outer(2 * s + core, l))

    def join(s):
        pair(s).wait_recv()

        def merge(_, l):
            mine, first = (block_rows(s, core), pl.ds(l, LANES)), core == 0
            theirs = (slice(None), pl.ds(l, LANES))
            own = [part[(c,) + mine] for c in range(3)]
            other = [peer[(s, c) + theirs] for c in range(3)]
            light = jnp.exp2(-rate * jnp.where(first, own[2], other[2]))
            for c in range(2):
                joint[(s, c) + theirs] = jnp.where(first, own[c], other[c]) + light * jnp.where(first, other[c], own[c])
            joint[(s, 2) + theirs] = own[2] + other[2]

        over(1, merge)
        for dx in FAR_FIRST:
            for m in range(2):
                j = 2 * lax.rem(x + dx, width) + lax.rem(lax.div(y, 2) + 1 + m, 2)
                pl.when(owner(s, j) != chip)(lambda: share(s, j).start())

        @pl.when(owns(s))
        def _():
            for c in range(3):
                shares[s, chip, c] = joint[s, c, :, tile_cols(own_tile)]

    def compose(s):
        @pl.when(owns(s))
        def _():
            await_tiles(share_recv.at[s], chips - 1)
            red, green, depth = (shares[s, 0, c] for c in range(3))
            for k in range(1, chips):
                light = jnp.exp2(-rate * depth)
                red, green = red + light * shares[s, k, 0], green + light * shares[s, k, 1]
                depth = depth + shares[s, k, 2]
            opacity = 1.0 - jnp.exp2(-rate * depth)
            for c, value in enumerate((0.5 * (opacity + red), green, opacity)):
                final[c, block_rows(s, core), tile_cols(own_tile)] = value
            for dx in FAR_FIRST:
                for dy in FAR_FIRST:
                    if dx or dy:
                        spread(s, lax.rem(x + dx, width) * width + lax.rem(y + dy, width)).start()

    def gather(s):
        pl.when(owns(s))(lambda: await_tiles(spread_recv.at[s], tiles - 1))
        pl.when(jnp.logical_not(owns(s)))(lambda: await_tiles(spread_recv.at[s], tiles))
        swap(s, core).start()

    def finish(s):
        swap(s, 1 - core).wait_recv()
        at = pl.ds(2 * s * ROWS, 2 * ROWS)
        red, green, opacity = (final[c, at] for c in range(3))
        for c, value in enumerate((red, green, opacity - red, opacity)):
            image[c, at] = value

    order = (1, 2, 0, 3)
    shade(order[0])
    for earlier, s in zip(order, order[1:]):
        shade(s)
        join(earlier)
    join(order[-1])
    for s in order:
        compose(s)
    gather(order[0])
    for earlier, s in zip(order, order[1:]):
        gather(s)
        finish(earlier)
    finish(order[-1])

    def sent(like, sem):
        pltpu.make_async_copy(like, like, sem).wait()

    for way in range(2):
        pl.when(d_to[way])(lambda: sent(now.at[pl.ds(0, 2), inner_rows, inner_cols], face_send.at[way]))
        pl.when(t_to[way])(lambda: sent(old.at[0, pl.ds(0, 2 * planes)], edge_send.at[way]))
    sent(peer, pair_send)
    await_tiles(share_send, PIECES * tiles - 2)
    await_tiles(spread_send, 2 * (chips - 1))
    sent(peer, swap_send)
    mid_store.wait()


def shards(pressure_old, pressure_now, solid_flags):
    planes, rows, cols = pressure_now.shape
    chips = lax.axis_size("depth") // 2
    any_space = pl.BlockSpec(memory_space=pl.ANY)
    f32 = jnp.float32
    halo = (planes + 2, rows + 2 * ROWS, cols + 2 * LANES)
    return pl.pallas_call(
        functools.partial(kernel, 4.0 / (planes * lax.axis_size("depth"))),
        out_shape=[
            jax.ShapeDtypeStruct(pressure_now.shape, f32),
            jax.ShapeDtypeStruct(pressure_now.shape, f32),
            jax.ShapeDtypeStruct((4, rows, cols), f32),
        ],
        in_specs=[any_space] * 3,
        out_specs=[pl.BlockSpec(memory_space=pltpu.VMEM)] * 3,
        scratch_shapes=[
            pltpu.VMEM(halo, f32),
            pltpu.VMEM(pressure_now.shape, f32),
            pltpu.VMEM(pressure_now.shape, jnp.int32),
            pltpu.VMEM(halo, f32),
            pltpu.VMEM((3, rows, cols), f32),
            pltpu.VMEM((PIECES, 3, ROWS, cols), f32),
            pltpu.VMEM((PIECES, 3, ROWS, cols), f32),
            pltpu.VMEM((PIECES, chips, 3, ROWS, LANES), f32),
            pltpu.VMEM((3, rows, cols), f32),
            pltpu.SemaphoreType.DMA((PIECES,)),
            pltpu.SemaphoreType.DMA,
            pltpu.SemaphoreType.DMA((2,)),
            pltpu.SemaphoreType.DMA((2, 2, PIECES)),
            pltpu.SemaphoreType.DMA((2,)),
            pltpu.SemaphoreType.DMA((2, 2)),
            pltpu.SemaphoreType.DMA,
            pltpu.SemaphoreType.DMA((PIECES,)),
            pltpu.SemaphoreType.DMA,
            pltpu.SemaphoreType.DMA((PIECES,)),
            pltpu.SemaphoreType.DMA,
            pltpu.SemaphoreType.DMA((PIECES,)),
            pltpu.SemaphoreType.DMA,
            pltpu.SemaphoreType.DMA((PIECES,)),
        ],
        compiler_params=pltpu.CompilerParams(
            collective_id=0, has_side_effects=True, vmem_limit_bytes=48 * 1024 * 1024
        ),
    )(pressure_now, pressure_old, solid_flags)


def solution(mesh):
    return jax.shard_map(
        shards,
        mesh=mesh,
        in_specs=(P("depth", "tile", None), P("depth", "tile", None), P("depth", "tile", None)),
        out_specs=(P("depth", "tile", None), P("depth", "tile", None), P(None, "tile", None)),
        check_vma=False,
    )
```
